512 devices in a mesh: dp: 32 (over x_hi, z), mp: 16 (over x_lo, y, core).
Axes of the slice: x: 4 (x_hi: 2, x_lo: 2; x = x_hi * 2 + x_lo), y: 4, z: 16, core: 2. Of those that a mesh axis runs over, the one named last changes fastest.
Arguments:
- captions: bfloat16 [65536, 1280], P(('dp', 'mp')), may hold values from -24 to 24
- audio: bfloat16 [512, 32, 1280], P(('dp', 'mp')), may hold values from -6 to 6
- caption_len: int32 [512], P('dp'), may hold values from 1 to 128
- pairing: int32 [32, 16], P('dp'), may hold values from 0 to 15, each once within a row
- enc_gain: float32 [1280], replicated, may hold values from 0.5 to 1.5
- enc_bias: float32 [1280], replicated, may hold values from -2.5 to 2.5
- dec_gain: float32 [1280], replicated, may hold values from 0.5 to 1.5
- dec_bias: float32 [1280], replicated, may hold values from -2.5 to 2.5
- w_query: bfloat16 [1280, 1024], P(None, 'mp'), may hold values from -0.15625 to 0.15625
- w_key: bfloat16 [1280, 1024], P(None, 'mp'), may hold values from -0.15625 to 0.15625
- w_value: bfloat16 [1280, 1024], P(None, 'mp'), may hold values from -0.15625 to 0.15625
- w_out: bfloat16 [1024, 1280], P('mp'), may hold values from -0.1875 to 0.1875
- grad_update: bfloat16 [65536, 1280], P(('dp', 'mp')), may hold values from -24 to 24
Outputs:
- cross_update: bfloat16 [65536, 1280], P(('dp', 'mp'))
- grad_captions: bfloat16 [65536, 1280], P(('dp', 'mp'))
- grad_audio: bfloat16 [512, 32, 1280], P(('dp', 'mp'))
- grad_wq: float32 [1280, 1024], P('dp', 'mp')
- grad_wo: float32 [1024, 1280], P('mp', 'dp')
The draws below stay inside these ranges and needn't reach their ends.
Inputs may be any that keep to these rules, and one draw needn't show every extreme that they name: Each row of pairing names each of the group's 16 clips exactly once.
All inputs are finite; a program needn't handle non-finite values.
Results may differ from the reference program's by a relative error of at most 0.024.
Values may be sent and summed in bfloat16 or wider, within the bound.
No kernel may reach another device: no remote copies, remote signals or barrier semaphores. Data moves between devices by JAX's collectives and lax.ppermute only.
A program may use at most 64 MiB of HBM per device.

```python
import math
import jax
import jax.numpy as jnp
from jax import lax

D = 1280
HEADS = 16
HEAD_DIM = 64
FRAMES = 32
CAP_LEN = 128
GROUPS = 32
GROUP_CLIPS = 16
CLIPS = 512
CAPTIONS = 512
TOKENS = 65536


def place_ends(array, key, least, largest):
    spot = [jax.random.randint(jax.random.fold_in(key, axis), (), 0, length) for axis, length in enumerate(array.shape)]
    longest = array.shape.index(max(array.shape))
    beside = spot[:longest] + [(spot[longest] + 1) % array.shape[longest]] + spot[longest + 1:]
    return array.at[tuple(spot)].set(least).at[tuple(beside)].set(largest)


def with_spikes(array, rng, source, target, shards_of, factor):
    owner, partner = [(jnp.arange(array.shape[dim]) // (array.shape[dim] // shards_of)).reshape([-1 if axis == dim else 1 for axis in range(array.ndim)]) for dim in (source, target)]
    chosen = jax.random.permutation(rng, shards_of)[partner]
    strong = (owner == chosen) | (owner == (partner + shards_of // 2) % shards_of)
    return jnp.where(strong, factor * array, array)


def levels(stream_key, shape, pieces, low, top_value):
    factor_of, own = 1.0, jax.random.fold_in(stream_key, 6)
    for dim, shards_of in pieces:
        draws = jnp.exp(jax.random.uniform(jax.random.fold_in(own, dim), (shards_of,), jnp.float32, low / len(pieces), top_value / len(pieces)))
        factor_of = factor_of * jnp.repeat(draws, shape[dim] // shards_of).reshape([-1 if axis == dim else 1 for axis in range(len(shape))])
    return factor_of


def gaussian(own_key, dims, scale, bound, pieces=(), held_as=jnp.bfloat16):
    values = jax.random.normal(own_key, dims, jnp.float32) * scale
    if len(pieces) > 0:
        values = levels(own_key, dims, pieces, -0.22, 0.18) * values
    return jnp.clip(values, min=-bound, max=bound).astype(held_as)


def bell_draw_with(key, extent, spread, reach, cuts, heavy, kind=jnp.bfloat16):
    entries = spread * jax.random.normal(key, extent, jnp.float32)
    if cuts:
        entries = entries * levels(key, extent, cuts, -0.22, 0.18)
    return jnp.clip(with_spikes(entries, jax.random.fold_in(key, 3), *heavy), -reach, reach).astype(kind)


def setup_inputs(seed: int = 0) -> dict:
    streams_of = jax.random.split(jax.random.key(seed), 14)
    return {
        "captions": bell_draw_with(streams_of[0], (TOKENS, D), 1.0, 24.0, ((0, 512),), (0, 1, 256, 6.0)),
        "audio": gaussian(streams_of[1], (CLIPS, FRAMES, D), 1.0, 6.0, ((0, 512),)),
        "caption_len": place_ends(jax.random.randint(streams_of[2], (CAPTIONS,), 1, CAP_LEN + 1), jax.random.fold_in(streams_of[2], 1), 1, CAP_LEN).astype(jnp.int32),
        "pairing": jax.vmap(lambda own: jax.random.permutation(own, GROUP_CLIPS))(jax.random.split(streams_of[3], GROUPS)).reshape((GROUPS, GROUP_CLIPS)).astype(jnp.int32),
        "enc_gain": jnp.clip(1.0 + 0.1 * jax.random.normal(streams_of[4], (D,), jnp.float32), 0.5, 1.5),
        "enc_bias": gaussian(streams_of[5], (D,), 0.5, 2.5, (), jnp.float32),
        "dec_gain": jnp.clip(1.0 + 0.1 * jax.random.normal(streams_of[6], (D,), jnp.float32), 0.5, 1.5),
        "dec_bias": gaussian(streams_of[7], (D,), 0.5, 2.5, (), jnp.float32),
        "w_query": gaussian(streams_of[8], (D, HEADS * HEAD_DIM), D ** -0.5, 0.15625, ((1, 16),)),
        "w_key": gaussian(streams_of[9], (D, HEADS * HEAD_DIM), D ** -0.5, 0.15625, ((1, 16),)),
        "w_value": gaussian(streams_of[10], (D, HEADS * HEAD_DIM), D ** -0.5, 0.15625, ((1, 16),)),
        "w_out": gaussian(streams_of[11], (HEADS * HEAD_DIM, D), (HEADS * HEAD_DIM) ** -0.5, 0.1875, ((0, 16),)),
        "grad_update": bell_draw_with(streams_of[12], (TOKENS, D), 1.0, 24.0, ((0, 512),), (0, 1, 256, 6.0)),
    }


EPSILON = 1e-05

def normalize(values, gain_vec, bias_vec):
    row_mean = lax.optimization_barrier(jnp.mean(values, axis=-1, keepdims=True))
    centred = values - row_mean
    inverse_std = lax.rsqrt(lax.optimization_barrier(jnp.mean(centred * centred, axis=-1, keepdims=True)) + EPSILON)
    normed = centred * inverse_std
    return (normed * gain_vec + bias_vec, normed, inverse_std)

def norm_backward(upstream, normed, inverse_std, gain_vec):
    scaled = upstream * gain_vec
    mean_term = lax.optimization_barrier(jnp.mean(scaled, axis=-1, keepdims=True))
    cross_term = lax.optimization_barrier(jnp.mean(scaled * normed, axis=-1, keepdims=True))
    return inverse_std * (scaled - mean_term - normed * cross_term)

def rounded(values):
    return lax.optimization_barrier(values.astype(jnp.bfloat16))

def shard_sum(left_rows, right_rows, shard_width):

    def add_shard(running, shard_index):
        left_part = lax.dynamic_slice_in_dim(left_rows, shard_index * shard_width, shard_width, 1)
        right_part = lax.dynamic_slice_in_dim(right_rows, shard_index * shard_width, shard_width, 0)
        partial_sum = rounded(jnp.dot(left_part, right_part, preferred_element_type=jnp.float32))
        return (running + partial_sum.astype(jnp.float32), None)
    start_value = jnp.zeros((left_rows.shape[0], right_rows.shape[1]), jnp.float32)
    return lax.scan(add_shard, start_value, jnp.arange(GROUP_CLIPS, dtype=jnp.int32))[0]

def reference(captions, audio, caption_len, pairing, enc_gain, enc_bias, dec_gain, dec_bias, w_query, w_key, w_value, w_out, grad_update):
    attn_width = HEADS * HEAD_DIM
    shard_width = attn_width // GROUP_CLIPS
    attn_scale = 1.0 / math.sqrt(HEAD_DIM)
    audio_rows = audio.reshape(CLIPS * FRAMES, D).astype(jnp.float32)
    state_values, state_normed, state_inverse = normalize(audio_rows, enc_gain, enc_bias)
    states = state_values.astype(jnp.bfloat16)
    caption_rows = captions.astype(jnp.float32)
    hidden_values, caption_normed, caption_inverse = normalize(caption_rows, dec_gain, dec_bias)
    hidden = hidden_values.astype(jnp.bfloat16)
    queries = rounded(jnp.dot(hidden, w_query, preferred_element_type=jnp.float32))
    five_shape = (GROUPS, GROUP_CLIPS, FRAMES, HEADS, HEAD_DIM)
    key_rows = rounded(jnp.dot(states, w_key, preferred_element_type=jnp.float32)).reshape(five_shape)
    value_rows = rounded(jnp.dot(states, w_value, preferred_element_type=jnp.float32)).reshape(five_shape)
    group_ids = jnp.arange(GROUPS, dtype=jnp.int32)
    key_sel = key_rows[group_ids[:, None], pairing].astype(jnp.float32)
    value_sel = value_rows[group_ids[:, None], pairing].astype(jnp.float32)
    query_five = queries.reshape(GROUPS, GROUP_CLIPS, CAP_LEN, HEADS, HEAD_DIM).astype(jnp.float32)
    scores = jnp.einsum('gclhe,gcfhe->gchlf', query_five, key_sel) * attn_scale
    weights = jnp.exp(scores)
    softmax = weights / lax.optimization_barrier(jnp.sum(weights, axis=-1, keepdims=True))
    softmax_low = rounded(softmax).astype(jnp.float32)
    attended = rounded(jnp.einsum('gchlf,gcfhe->gclhe', softmax_low, value_sel)).reshape(TOKENS, attn_width)
    cross_update = shard_sum(attended, w_out, shard_width).astype(jnp.bfloat16)
    positions = jnp.arange(CAP_LEN, dtype=jnp.int32)
    live_rows = (positions[None, :] < caption_len[:, None]).reshape(TOKENS, 1)
    upstream = jnp.where(live_rows, grad_update, jnp.zeros_like(grad_update))
    d_attended = rounded(jnp.dot(upstream, w_out.T, preferred_element_type=jnp.float32))
    grad_wo = jnp.dot(attended.T, upstream, preferred_element_type=jnp.float32)
    d_att_five = d_attended.reshape(GROUPS, GROUP_CLIPS, CAP_LEN, HEADS, HEAD_DIM).astype(jnp.float32)
    d_softmax = jnp.einsum('gclhe,gcfhe->gchlf', d_att_five, value_sel)
    d_scores = rounded(softmax * (d_softmax - lax.optimization_barrier(jnp.sum(softmax * d_softmax, axis=-1, keepdims=True))) * attn_scale).astype(jnp.float32)
    d_queries = rounded(jnp.einsum('gchlf,gcfhe->gclhe', d_scores, key_sel)).reshape(TOKENS, attn_width)
    d_key_sel = rounded(jnp.einsum('gchlf,gclhe->gcfhe', d_scores, query_five))
    d_value_sel = rounded(jnp.einsum('gchlf,gclhe->gcfhe', softmax_low, d_att_five))
    d_keys = jnp.zeros(five_shape, jnp.bfloat16).at[group_ids[:, None], pairing].set(d_key_sel)
    d_values = jnp.zeros(five_shape, jnp.bfloat16).at[group_ids[:, None], pairing].set(d_value_sel)
    d_keys = d_keys.reshape(CLIPS * FRAMES, attn_width)
    d_values = d_values.reshape(CLIPS * FRAMES, attn_width)
    d_states = jnp.dot(d_keys, w_key.T, preferred_element_type=jnp.float32) + jnp.dot(d_values, w_value.T, preferred_element_type=jnp.float32)
    grad_audio = norm_backward(d_states, state_normed, state_inverse, enc_gain).astype(jnp.bfloat16).reshape(CLIPS, FRAMES, D)
    d_hidden = shard_sum(d_queries, w_query.T, shard_width)
    grad_captions = norm_backward(d_hidden, caption_normed, caption_inverse, dec_gain).astype(jnp.bfloat16)
    grad_wq = jnp.dot(hidden.T, d_queries, preferred_element_type=jnp.float32)
    return (cross_update, grad_captions, grad_audio, grad_wq, grad_wo)
```

```python
import functools
import math

import jax
import jax.numpy as jnp
from jax import lax
from jax.experimental import pallas as pl
from jax.experimental.pallas import tpu as pltpu
from jax.sharding import PartitionSpec as P

HEAD_DIM = 64
EPSILON = 1e-05
FRAMES = 32
CAP = 128
HELD = 4
ROWS = HELD * CAP
WIDTH = HELD * HEAD_DIM
BF16 = jnp.bfloat16
F32 = jnp.float32
LARGEST_BF16 = 3.3895313892515355e38

VMEM = pl.BlockSpec(memory_space=pltpu.VMEM)
SMEM = pl.BlockSpec(memory_space=pltpu.SMEM)
MIB = 1 << 20


def params(mib):
    return pltpu.CompilerParams(vmem_limit_bytes=mib * MIB)


def dot(left, right, left_dim=1, right_dim=0):
    return lax.dot_general(
        left, right, (((left_dim,), (right_dim,)), ((), ())), preferred_element_type=F32
    )


def standardize(values):
    row_mean = jnp.mean(values, axis=-1, keepdims=True)
    centred = values - row_mean
    inverse_std = lax.rsqrt(jnp.mean(centred * centred, axis=-1, keepdims=True) + EPSILON)
    return centred * inverse_std, inverse_std


def norm_backward(upstream, normed, inverse_std, gain_vec):
    scaled = upstream * gain_vec
    mean_term = jnp.mean(scaled, axis=-1, keepdims=True)
    cross_term = jnp.mean(scaled * normed, axis=-1, keepdims=True)
    return inverse_std * (scaled - mean_term - normed * cross_term)


def held_caption(own, part):
    return own ^ ((part & 1) * 8) ^ (part >> 1)


def pack_kernel(wq_ref, wk_ref, wv_ref, wo_ref, out_ref):
    for kind, block in enumerate((wq_ref[...].T, wk_ref[...].T, wv_ref[...].T, wo_ref[...])):
        for target in range(out_ref.shape[0]):
            out_ref[target, kind * HEAD_DIM : (kind + 1) * HEAD_DIM, :] = block


def weight_of(w_ref, kind):
    rows = w_ref[:, kind * HEAD_DIM : (kind + 1) * HEAD_DIM, :]
    return rows.reshape(WIDTH, w_ref.shape[2])


def project_kernel(own_ref, len_ref, t0, t1, t2, t3, gain, bias, w_ref, hid_ref, up_ref, q_ref, da_ref):
    own = own_ref[0]
    positions = lax.broadcasted_iota(jnp.int32, (CAP, 1), 0)
    for part, tokens in enumerate((t0, t1, t2, t3)):
        span = slice(part * CAP, (part + 1) * CAP)
        normed, _ = standardize(tokens[0].astype(F32))
        hid_ref[span, :] = (normed * gain[...] + bias[...]).astype(BF16)
        live = positions < len_ref[held_caption(own, part)]
        up_ref[span, :] = jnp.where(live, tokens[1].astype(F32), 0.0).astype(BF16)
    q_ref[...] = dot(hid_ref[...], weight_of(w_ref, 0), 1, 1).astype(BF16)
    da_ref[...] = dot(up_ref[...], weight_of(w_ref, 3), 1, 1).astype(BF16)


def segment_sum(values, ones):
    high = jnp.minimum(values, LARGEST_BF16).astype(BF16)
    low = (values - high.astype(F32)).astype(BF16)
    return dot(high, ones) + dot(low, ones)


def attend_kernel(
    own_ref, pair_ref, audio_ref, gain, bias, w_ref, q_ref, da_ref, att_ref, dq_ref, ds_ref, st_ref, dk_ref, dv_ref
):
    own = own_ref[0]
    scale = 1.0 / math.sqrt(HEAD_DIM)
    for part in range(HELD):
        clip = pair_ref[0, held_caption(own, part)]
        normed, _ = standardize(audio_ref[clip].astype(F32))
        st_ref[part * FRAMES : (part + 1) * FRAMES, :] = (normed * gain[...] + bias[...]).astype(BF16)
    keys = dot(st_ref[...], weight_of(w_ref, 1), 1, 1).astype(BF16)
    values = dot(st_ref[...], weight_of(w_ref, 2), 1, 1).astype(BF16)
    pairs = HELD * FRAMES
    row_head = lax.broadcasted_iota(jnp.int32, (pairs, WIDTH), 0) // FRAMES
    lane_head = lax.broadcasted_iota(jnp.int32, (pairs, WIDTH), 1) // HEAD_DIM
    same = row_head == lane_head
    first = lax.broadcasted_iota(jnp.int32, (pairs, pairs), 0) // FRAMES
    second = lax.broadcasted_iota(jnp.int32, (pairs, pairs), 1) // FRAMES
    ones = jnp.where(first == second, 1.0, 0.0).astype(BF16)

    def spread(rows):
        repeated = jnp.concatenate([rows.astype(F32)] * HELD, axis=0)
        return jnp.where(same, repeated, 0.0).astype(BF16)

    def gather(rows):
        kept = jnp.where(same, rows, 0.0)
        total = kept[0:FRAMES]
        for head in range(1, HELD):
            total = total + kept[head * FRAMES : (head + 1) * FRAMES]
        return total.astype(BF16)

    for part in range(HELD):
        span = slice(part * CAP, (part + 1) * CAP)
        frames = slice(part * FRAMES, (part + 1) * FRAMES)
        key_block = spread(keys[frames])
        value_block = spread(values[frames])
        query = q_ref[span, :]
        d_att = da_ref[span, :]
        weights = jnp.exp(dot(query, key_block, 1, 1) * scale)
        softmax = weights / segment_sum(weights, ones)
        low = softmax.astype(BF16)
        att_ref[span, :] = dot(low, value_block).astype(BF16)
        d_softmax = dot(d_att, value_block, 1, 1)
        inner = segment_sum(softmax * d_softmax, ones)
        d_scores = (softmax * (d_softmax - inner) * scale).astype(BF16)
        dq_ref[span, :] = dot(d_scores, key_block).astype(BF16)
        dk_ref[frames, :] = gather(dot(d_scores, query, 0, 0))
        dv_ref[frames, :] = gather(dot(low, d_att, 0, 0))
    ds_ref[...] = (
        dot(dk_ref[...], weight_of(w_ref, 1)) + dot(dv_ref[...], weight_of(w_ref, 2))
    ).astype(BF16)


def update_kernel(w_ref, att_ref, dq_ref, keep_ref, send_ref):
    w_out = weight_of(w_ref, 3)
    w_query = weight_of(w_ref, 0)
    for part in range(HELD):
        span = slice(part * CAP, (part + 1) * CAP)
        target = send_ref if part >> 1 else keep_ref
        target[part & 1, 0] = dot(att_ref[span, :], w_out).astype(BF16)
        target[part & 1, 1] = dot(dq_ref[span, :], w_query).astype(BF16)


def weight_grad_kernel(hid_ref, up_ref, att_ref, dq_ref, grad_ref):
    half = hid_ref.shape[1] // 2
    for kind, (left, right) in enumerate(((dq_ref, hid_ref), (att_ref, up_ref))):
        product = dot(left[...], right[...], 0, 0).astype(BF16)
        for side in range(2):
            for head in range(HELD):
                grad_ref[side * HELD + head, kind * HEAD_DIM : (kind + 1) * HEAD_DIM, :] = product[
                    head * HEAD_DIM : (head + 1) * HEAD_DIM, side * half : (side + 1) * half
                ]


def grad_sum_kernel(parts_ref, out_ref):
    total = parts_ref[0].astype(F32)
    for part in range(1, parts_ref.shape[0]):
        total = total + parts_ref[part].astype(F32)
    out_ref[...] = total.T.astype(BF16)


def grad_final_kernel(parts_ref, wq_ref, wo_ref):
    total = parts_ref[0].astype(F32)
    for part in range(1, parts_ref.shape[0]):
        total = total + parts_ref[part].astype(F32)
    wq_ref[...] = total[:, :HEAD_DIM]
    wo_ref[...] = total[:, HEAD_DIM:].T


def caption_final_kernel(keep_ref, core_ref, x_ref, caption_ref, gain, update_ref, grad_ref):
    def total(kind):
        near = keep_ref[0, kind].astype(F32) + core_ref[0, kind].astype(F32)
        return near + x_ref[kind].astype(F32)

    update_ref[...] = total(0).astype(BF16)
    normed, inverse_std = standardize(caption_ref[...].astype(F32))
    grad_ref[...] = norm_backward(total(1), normed, inverse_std, gain[...]).astype(BF16)


def audio_final_kernel(own_ref, pair_ref, p0, p1, p2, p3, audio_ref, gain, out_ref):
    del own_ref, pair_ref
    total = (p0[0].astype(F32) + p1[0].astype(F32)) + (p2[0].astype(F32) + p3[0].astype(F32))
    normed, inverse_std = standardize(audio_ref[0].astype(F32))
    out_ref[0] = norm_backward(total, normed, inverse_std, gain[...]).astype(BF16)


def describing_block(part, step, own_ref, pair_ref):
    del step
    caption = 0
    for index in range(pair_ref.shape[1]):
        caption = jnp.where(pair_ref[0, index] == own_ref[0], index, caption)
    return held_caption(caption, part) * HELD + part, 0, 0


def body(
    captions,
    audio,
    caption_len,
    pairing,
    enc_gain,
    enc_bias,
    dec_gain,
    dec_bias,
    w_query,
    w_key,
    w_value,
    w_out,
    grad_update,
    *,
    depth,
    y_groups,
    yx_groups,
    z_groups,
):
    both = ("dp", "mp")
    width = captions.shape[1]
    shape = jax.ShapeDtypeStruct
    own = lax.axis_index("mp").astype(jnp.int32).reshape(1)
    enc_gain, enc_bias, dec_gain, dec_bias = (
        vector.reshape(1, width) for vector in (enc_gain, enc_bias, dec_gain, dec_bias)
    )
    swap_core = [(index, index ^ 1) for index in range(16)]
    swap_x = [(index, index ^ 8) for index in range(16)]

    audio_all = lax.all_gather(audio, "mp", axis=0, tiled=True)
    tokens_own = jnp.stack([captions, grad_update])
    tokens_x = lax.ppermute(tokens_own, "mp", swap_x)
    tokens_core = lax.ppermute(tokens_own, "mp", swap_core)
    tokens_far = lax.ppermute(tokens_x, "mp", swap_core)

    packed = pl.pallas_call(
        pack_kernel,
        out_shape=shape((HELD, 4 * HEAD_DIM, width), BF16),
        in_specs=[VMEM] * 4,
        out_specs=VMEM,
        compiler_params=params(16),
        name="pack_weights",
    )(w_query, w_key, w_value, w_out)
    weights = lax.all_to_all(packed, "mp", 0, 0, axis_index_groups=y_groups, tiled=True)

    hidden, upstream, queries, d_attended = pl.pallas_call(
        project_kernel,
        out_shape=(
            shape((ROWS, width), BF16),
            shape((ROWS, width), BF16),
            shape((ROWS, WIDTH), BF16),
            shape((ROWS, WIDTH), BF16),
        ),
        in_specs=[SMEM, SMEM] + [VMEM] * 7,
        out_specs=(VMEM,) * 4,
        compiler_params=params(32),
        name="project",
    )(own, caption_len, tokens_own, tokens_x, tokens_core, tokens_far, dec_gain, dec_bias, weights)

    attended, d_queries, d_states = pl.pallas_call(
        attend_kernel,
        out_shape=(
            shape((ROWS, WIDTH), BF16),
            shape((ROWS, WIDTH), BF16),
            shape((HELD * FRAMES, width), BF16),
        ),
        in_specs=[SMEM, SMEM] + [VMEM] * 6,
        out_specs=(VMEM,) * 3,
        scratch_shapes=[
            pltpu.VMEM((HELD * FRAMES, width), BF16),
            pltpu.VMEM((HELD * FRAMES, WIDTH), BF16),
            pltpu.VMEM((HELD * FRAMES, WIDTH), BF16),
        ],
        compiler_params=params(32),
        name="attend",
    )(own, pairing, audio_all, enc_gain, enc_bias, weights, queries, d_attended)

    states_all = lax.all_gather(d_states, "mp", axis=0, tiled=True)

    weight_parts = pl.pallas_call(
        weight_grad_kernel,
        out_shape=shape((2 * HELD, 2 * HEAD_DIM, width // 2), BF16),
        in_specs=[VMEM] * 4,
        out_specs=VMEM,
        compiler_params=params(32),
        name="weight_grads",
    )(hidden, upstream, attended, d_queries)
    weight_parts = lax.all_to_all(
        weight_parts, both, 0, 0, axis_index_groups=yx_groups, tiled=True
    )

    keep, send = pl.pallas_call(
        update_kernel,
        out_shape=(shape((2, 2, CAP, width), BF16),) * 2,
        in_specs=[VMEM] * 3,
        out_specs=(VMEM,) * 2,
        compiler_params=params(32),
        name="updates",
    )(weights, attended, d_queries)
    core_parts = lax.ppermute(send, "mp", swap_core)
    x_send = (keep[1].astype(F32) + core_parts[1].astype(F32)).astype(BF16)
    x_parts = lax.ppermute(x_send, "mp", swap_x)

    weight_half = pl.pallas_call(
        grad_sum_kernel,
        out_shape=shape((width // 2, 2 * HEAD_DIM), BF16),
        in_specs=[VMEM],
        out_specs=VMEM,
        compiler_params=params(16),
        name="sum_weight_grads",
    )(weight_parts)
    weight_last = lax.all_to_all(
        weight_half.reshape(depth, width // (2 * depth), 2 * HEAD_DIM),
        both,
        0,
        0,
        axis_index_groups=z_groups,
        tiled=True,
    )
    grad_wq, grad_wo = pl.pallas_call(
        grad_final_kernel,
        out_shape=(
            shape((width // (2 * depth), HEAD_DIM), F32),
            shape((HEAD_DIM, width // (2 * depth)), F32),
        ),
        in_specs=[VMEM],
        out_specs=(VMEM,) * 2,
        compiler_params=params(16),
        name="final_weight_grads",
    )(weight_last)

    near = pl.BlockSpec((1, 2, CAP, width), lambda step: (0, 0, 0, 0))
    cross_update, grad_captions = pl.pallas_call(
        caption_final_kernel,
        grid=(1,),
        out_shape=(shape((CAP, width), BF16),) * 2,
        in_specs=[
            near,
            near,
            pl.BlockSpec((2, CAP, width), lambda step: (0, 0, 0)),
            pl.BlockSpec((CAP, width), lambda step: (0, 0)),
            pl.BlockSpec((1, width), lambda step: (0, 0)),
        ],
        out_specs=(pl.BlockSpec((CAP, width), lambda step: (0, 0)),) * 2,
        compiler_params=params(16),
        name="final_captions",
    )(keep, core_parts, x_parts, captions, dec_gain)

    state_blocks = states_all.reshape(-1, FRAMES, width)
    grad_audio = pl.pallas_call(
        audio_final_kernel,
        grid_spec=pltpu.PrefetchScalarGridSpec(
            num_scalar_prefetch=2,
            grid=(1,),
            in_specs=[
                pl.BlockSpec((1, FRAMES, width), functools.partial(describing_block, part))
                for part in range(HELD)
            ]
            + [
                pl.BlockSpec((1, FRAMES, width), lambda step, own_ref, pair_ref: (0, 0, 0)),
                pl.BlockSpec((1, width), lambda step, own_ref, pair_ref: (0, 0)),
            ],
            out_specs=pl.BlockSpec((1, FRAMES, width), lambda step, own_ref, pair_ref: (0, 0, 0)),
        ),
        out_shape=shape((1, FRAMES, width), BF16),
        compiler_params=params(16),
        name="final_audio",
    )(own, pairing, *([state_blocks] * HELD), audio, enc_gain)

    return (cross_update, grad_captions, grad_audio, grad_wq, grad_wo)


def device_groups(dp_size):
    depth = dp_size // 2

    def device(x_hi, z, x_lo, y, core):
        return (x_hi * depth + z) * 16 + (x_lo * 4 + y) * 2 + core

    y_groups = [[(x * 4 + y) * 2 + core for y in range(4)] for x in range(2) for core in range(2)]
    yx_groups = [
        [device(x_hi, z, x_lo, y, core) for x_hi in range(2) for y in range(4)]
        for z in range(depth)
        for x_lo in range(2)
        for core in range(2)
    ]
    z_groups = [
        [device(x_hi, z, x_lo, y, core) for z in range(depth)]
        for x_hi in range(2)
        for x_lo in range(2)
        for y in range(4)
        for core in range(2)
    ]
    return dict(depth=depth, y_groups=y_groups, yx_groups=yx_groups, z_groups=z_groups)


def solution(mesh):
    in_specs = (
        P(("dp", "mp"), None),
        P(("dp", "mp"), None, None),
        P("dp"),
        P("dp", None),
        P(),
        P(),
        P(),
        P(),
        P(None, "mp"),
        P(None, "mp"),
        P(None, "mp"),
        P("mp", None),
        P(("dp", "mp"), None),
    )
    out_specs = (
        P(("dp", "mp"), None),
        P(("dp", "mp"), None),
        P(("dp", "mp"), None, None),
        P("dp", "mp"),
        P("mp", "dp"),
    )
    local = functools.partial(body, **device_groups(mesh.shape["dp"]))
    return jax.shard_map(local, mesh=mesh, in_specs=in_specs, out_specs=out_specs, check_vma=False)
```

```python
import functools
import math

import jax
import jax.numpy as jnp
from jax import lax
from jax.experimental import pallas as pl
from jax.experimental.pallas import tpu as pltpu
from jax.sharding import PartitionSpec as P

HEAD_DIM = 64
EPSILON = 1e-05
FRAMES = 32
CAP = 128
HELD = 4
ROWS = HELD * CAP
WIDTH = HELD * HEAD_DIM
BF16 = jnp.bfloat16
F32 = jnp.float32
LARGEST_BF16 = 3.3895313892515355e38

HBM = pl.BlockSpec(memory_space=pltpu.HBM)
MIB = 1 << 20
BIG = 60
COST = pl.CostEstimate(flops=1000, bytes_accessed=1000, transcendentals=0)


def params(mib):
    return pltpu.CompilerParams(vmem_limit_bytes=mib * MIB)


def dot(left, right, left_dim=1, right_dim=0):
    return lax.dot_general(
        left, right, (((left_dim,), (right_dim,)), ((), ())), preferred_element_type=F32
    )


def standardize(values):
    row_mean = jnp.mean(values, axis=-1, keepdims=True)
    centred = values - row_mean
    inverse_std = lax.rsqrt(jnp.mean(centred * centred, axis=-1, keepdims=True) + EPSILON)
    return centred * inverse_std, inverse_std


def norm_backward(upstream, normed, inverse_std, gain_vec):
    scaled = upstream * gain_vec
    mean_term = jnp.mean(scaled, axis=-1, keepdims=True)
    cross_term = jnp.mean(scaled * normed, axis=-1, keepdims=True)
    return inverse_std * (scaled - mean_term - normed * cross_term)


def held_caption(own, part):
    return own ^ ((part & 1) * 8) ^ (part >> 1)


def caption_length(meta, caption):
    return meta[1 + caption]


def described_clip(meta, caption):
    return meta[17 + caption]


def row_of_y(own):
    return (own >> 1) & 3


def weight_of(w_ref, kind):
    rows = w_ref[:, kind * HEAD_DIM : (kind + 1) * HEAD_DIM, :]
    return rows.reshape(WIDTH, w_ref.shape[2])


def pack_kernel(io, *refs):
    *blocks, out_ref = refs
    io.take()
    first = 0
    for block in blocks:
        for target in range(HELD):
            out_ref[target, first : first + block.shape[0], :] = block[...]
        first += block.shape[0]


def norm_kernel(io, meta, t0, t1, t2, t3, gain, bias, hid_ref, up_ref):
    width = hid_ref.shape[1]
    io.take(0, 5, 6)
    own = meta[0]
    positions = lax.broadcasted_iota(jnp.int32, (CAP, 1), 0)
    gain_row, bias_row = gain[...].reshape(1, width), bias[...].reshape(1, width)
    for part, tokens in enumerate((t0, t1, t2, t3)):
        io.take(1 + part)
        span = slice(part * CAP, (part + 1) * CAP)
        normed, _ = standardize(tokens[0].astype(F32))
        hid_ref[span, :] = (normed * gain_row + bias_row).astype(BF16)
        live = positions < caption_length(meta, held_caption(own, part))
        up_ref[span, :] = jnp.where(live, tokens[1].astype(F32), 0.0).astype(BF16)


def segment_sum(values, ones):
    high = jnp.minimum(values, LARGEST_BF16).astype(BF16)
    low = (values - high.astype(F32)).astype(BF16)
    return dot(high, ones) + dot(low, ones)


def attend_kernel(
    io,
    meta,
    gain,
    bias,
    kv_ref,
    qo_ref,
    hid_ref,
    up_ref,
    near_ref,
    other_ref,
    dkv_ref,
    att_ref,
    dq_ref,
    states_ref,
):
    width = hid_ref.shape[1]
    io.take(0, 1, 2, 7, 8)
    own = meta[0]
    gain_row, bias_row = gain[...].reshape(1, width), bias[...].reshape(1, width)
    for part in range(HELD):
        clip = described_clip(meta, held_caption(own, part))
        place = row_of_y(clip) + 4 * ((clip ^ own) >> 3)
        near = ((clip ^ own) & 1) == 0
        frames = jnp.where(near, near_ref[place].astype(F32), other_ref[place].astype(F32))
        normed, _ = standardize(frames)
        states_ref[part * FRAMES : (part + 1) * FRAMES, :] = (normed * gain_row + bias_row).astype(BF16)
    io.take(3)
    keys = dot(states_ref[...], weight_of(kv_ref, 0), 1, 1).astype(BF16)
    values = dot(states_ref[...], weight_of(kv_ref, 1), 1, 1).astype(BF16)
    io.take(4, 5, 6)
    queries = dot(hid_ref[...], weight_of(qo_ref, 0), 1, 1).astype(BF16)
    d_attended = dot(up_ref[...], weight_of(qo_ref, 1), 1, 1).astype(BF16)
    scale = 1.0 / math.sqrt(HEAD_DIM)
    pairs = HELD * FRAMES
    row_head = lax.broadcasted_iota(jnp.int32, (pairs, WIDTH), 0) // FRAMES
    lane_head = lax.broadcasted_iota(jnp.int32, (pairs, WIDTH), 1) // HEAD_DIM
    same = row_head == lane_head
    first = lax.broadcasted_iota(jnp.int32, (pairs, pairs), 0) // FRAMES
    second = lax.broadcasted_iota(jnp.int32, (pairs, pairs), 1) // FRAMES
    ones = jnp.where(first == second, 1.0, 0.0).astype(BF16)

    def spread(rows):
        repeated = jnp.concatenate([rows.astype(F32)] * HELD, axis=0)
        return jnp.where(same, repeated, 0.0).astype(BF16)

    def collect(rows):
        kept = jnp.where(same, rows, 0.0)
        total = kept[0:FRAMES]
        for head in range(1, HELD):
            total = total + kept[head * FRAMES : (head + 1) * FRAMES]
        return total.astype(BF16)

    for part in range(HELD):
        span = slice(part * CAP, (part + 1) * CAP)
        frames = slice(part * FRAMES, (part + 1) * FRAMES)
        key_block, value_block = spread(keys[frames]), spread(values[frames])
        query = queries[span]
        d_att = d_attended[span]
        weights = jnp.exp(dot(query, key_block, 1, 1) * scale)
        softmax = weights / segment_sum(weights, ones)
        low = softmax.astype(BF16)
        att_ref[span, :] = dot(low, value_block).astype(BF16)
        d_softmax = dot(d_att, value_block, 1, 1)
        inner = segment_sum(softmax * d_softmax, ones)
        d_scores = (softmax * (d_softmax - inner) * scale).astype(BF16)
        dq_ref[span, :] = dot(d_scores, key_block).astype(BF16)
        d_keys = collect(dot(d_scores, query, 0, 0))
        d_values = collect(dot(low, d_att, 0, 0))
        for row in range(HELD):
            dkv_ref[row, 0, part] = d_keys
            dkv_ref[row, 1, part] = d_values


def weight_grad_kernel(io, att_ref, dq_ref, hid_ref, up_ref, grad_ref):
    io.take()
    half = hid_ref.shape[1] // 2
    for kind, (left, right) in enumerate(((dq_ref, hid_ref), (att_ref, up_ref))):
        for side in range(2):
            product = dot(left[...], right[:, side * half : (side + 1) * half], 0, 0).astype(BF16)
            for head in range(HELD):
                grad_ref[side * HELD + head, kind * HEAD_DIM : (kind + 1) * HEAD_DIM, :] = product[
                    head * HEAD_DIM : (head + 1) * HEAD_DIM
                ]


def update_kernel(io, meta, got_ref, att_ref, dq_ref, kv_ref, qo_ref, send_x, send_own, keep_ref, keys_ref, values_ref):
    io.take()
    own = meta[0]
    for part in range(HELD):
        clip = held_caption(own, part)
        caption = 0
        for index in range(4 * HELD):
            caption = jnp.where(described_clip(meta, index) == clip, index, caption)
        row = row_of_y(caption)
        apart = caption ^ own
        place = (apart >> 3) + 2 * (apart & 1)
        keys_ref[part * FRAMES : (part + 1) * FRAMES, :] = got_ref[row, 0, place]
        values_ref[part * FRAMES : (part + 1) * FRAMES, :] = got_ref[row, 1, place]
    w_query, w_out = weight_of(qo_ref, 0), weight_of(qo_ref, 1)
    d_states = dot(keys_ref[...], weight_of(kv_ref, 0)) + dot(values_ref[...], weight_of(kv_ref, 1))
    for part in reversed(range(HELD)):
        target = (keep_ref.at[0], keep_ref.at[1], send_own, send_x)[part]
        span = slice(part * CAP, (part + 1) * CAP)
        target[:CAP, :] = dot(att_ref[span, :], w_out).astype(BF16)
        target[CAP : 2 * CAP, :] = dot(dq_ref[span, :], w_query).astype(BF16)
        target[2 * CAP :, :] = d_states[part * FRAMES : (part + 1) * FRAMES].astype(BF16)
        if part > 1:
            io.give(3 - part)


def grad_sum_kernel(io, parts_ref, out_ref):
    io.take()
    total = parts_ref[0].astype(F32)
    for part in range(1, parts_ref.shape[0]):
        total = total + parts_ref[part].astype(F32)
    out_ref[...] = total.T.astype(BF16)


def grad_final_kernel(parts_ref, wq_ref, wo_ref):
    total = parts_ref[0].astype(F32)
    for part in range(1, parts_ref.shape[0]):
        total = total + parts_ref[part].astype(F32)
    wq_ref[...] = total[:, :HEAD_DIM]
    wo_ref[...] = total[:, HEAD_DIM:]


def add_kernel(io, left_ref, right_ref, out_ref):
    io.take()
    out_ref[...] = (left_ref[...].astype(F32) + right_ref[...].astype(F32)).astype(BF16)


def final_kernel(
    io, keep_ref, core_ref, x_ref, caption_ref, dec_gain, audio_ref, enc_gain, update_ref, grad_ref, out_ref
):
    io.take()
    width = caption_ref.shape[1]

    def total(start, stop):
        near = keep_ref[start:stop].astype(F32) + core_ref[start:stop].astype(F32)
        return near + x_ref[start:stop].astype(F32)

    update_ref[...] = total(0, CAP).astype(BF16)
    io.give(0)
    normed, inverse_std = standardize(caption_ref[...].astype(F32))
    d_hidden = total(CAP, 2 * CAP)
    grad_ref[...] = norm_backward(d_hidden, normed, inverse_std, dec_gain[...].reshape(1, width)).astype(BF16)
    io.give(1)
    normed, inverse_std = standardize(audio_ref[0].astype(F32))
    d_states = total(2 * CAP, 2 * CAP + FRAMES)
    out_ref[0] = norm_backward(d_states, normed, inverse_std, enc_gain[...].reshape(1, width)).astype(BF16)


class Transfers:
    def __init__(self, takes, gives):
        self.takes, self.gives = dict(enumerate(takes)), dict(enumerate(gives))
        self.given = []
        for copy in takes:
            copy.start()

    def take(self, *places):
        for place in places or tuple(self.takes):
            self.takes.pop(place).wait()

    def give(self, *places):
        for place in places or tuple(self.gives):
            self.given.append(self.gives.pop(place))
            self.given[-1].start()

    def finish(self):
        if self.gives:
            self.give()
        for copy in self.given:
            copy.wait()


def call(kernel, name, outs, operands, mib=BIG, scratch=(), scalars=0):
    takes, gives = len(operands), len(outs)
    places = [operand[1] if isinstance(operand, tuple) else None for operand in operands]
    operands = [operand[0] if isinstance(operand, tuple) else operand for operand in operands]

    def copied(*refs):
        given, wanted, refs = refs[:takes], refs[takes : takes + gives], refs[takes + gives :]
        held, made, refs = refs[:takes], refs[takes : takes + gives], refs[takes + gives :]
        sems, rest = refs[0], refs[1:]
        io = Transfers(
            [
                pltpu.make_async_copy(
                    given[i] if places[i] is None else given[i].at[places[i]], held[i], sems.at[i]
                )
                for i in range(takes)
            ],
            [pltpu.make_async_copy(made[i], wanted[i], sems.at[takes + i]) for i in range(gives)],
        )
        kernel(io, *held, *made, *rest)
        io.finish()

    def space(place, array):
        shape = array.shape if places[place] is None else array.shape[1:]
        return (pltpu.SMEM if place < scalars else pltpu.VMEM)(shape, array.dtype)

    return pl.pallas_call(
        copied,
        out_shape=tuple(jax.ShapeDtypeStruct(*out) for out in outs),
        in_specs=[HBM] * takes,
        out_specs=(HBM,) * gives,
        scratch_shapes=[space(place, operand) for place, operand in enumerate(operands)]
        + [pltpu.VMEM(*out) for out in outs]
        + [pltpu.SemaphoreType.DMA((takes + gives,))]
        + list(scratch),
        compiler_params=params(mib),
        cost_estimate=COST,
        name=name,
    )(*operands)


def body(
    captions,
    audio,
    caption_len,
    pairing,
    enc_gain,
    enc_bias,
    dec_gain,
    dec_bias,
    w_query,
    w_key,
    w_value,
    w_out,
    grad_update,
    *,
    depth,
    y_groups,
    yx_groups,
    z_groups,
):
    both = ("dp", "mp")
    width = captions.shape[1]
    own = lax.axis_index("mp").astype(jnp.int32).reshape(1)
    meta = jnp.concatenate([own, caption_len, pairing[0], jnp.zeros((95,), jnp.int32)])
    swap_core = [(index, index ^ 1) for index in range(16)]
    swap_x = [(index, index ^ 8) for index in range(16)]

    (kv_out,) = call(
        pack_kernel,
        "pack_keys_values",
        [((HELD, 2 * HEAD_DIM + FRAMES, width), BF16)],
        (w_key.T, w_value.T, (audio, 0)),
    )
    kv_got = lax.all_to_all(kv_out, "mp", 0, 0, axis_index_groups=y_groups, tiled=True)
    (qo_out,) = call(
        pack_kernel, "pack_queries_out", [((HELD, 2 * HEAD_DIM, width), BF16)], (w_query.T, w_out)
    )
    kv_got, qo_out = lax.optimization_barrier((kv_got, qo_out))
    qo_got = lax.all_to_all(qo_out, "mp", 0, 0, axis_index_groups=y_groups, tiled=True)
    audio_y = kv_got[:, 2 * HEAD_DIM :]
    audio_near = jnp.concatenate([audio_y, lax.ppermute(audio_y, "mp", swap_x)])
    audio_other = lax.ppermute(audio_near, "mp", swap_core)
    tokens_own = jnp.stack([captions, grad_update])
    tokens_x = lax.ppermute(tokens_own, "mp", swap_x)
    tokens_core = lax.ppermute(tokens_own, "mp", swap_core)
    tokens_far = lax.ppermute(tokens_x, "mp", swap_core)
    hidden, upstream = call(
        norm_kernel,
        "norms",
        [((ROWS, width), BF16), ((ROWS, width), BF16)],
        (meta, tokens_own, tokens_x, tokens_core, tokens_far, dec_gain, dec_bias),
        scalars=1,
    )

    d_kv, attended, d_queries = call(
        attend_kernel,
        "attend",
        [
            ((HELD, 2, HELD, FRAMES, WIDTH), BF16),
            ((ROWS, WIDTH), BF16),
            ((ROWS, WIDTH), BF16),
        ],
        (meta, enc_gain, enc_bias, kv_got, qo_got, hidden, upstream, audio_near, audio_other),
        scratch=[pltpu.VMEM((HELD * FRAMES, width), BF16)],
        scalars=1,
    )
    d_kv_got = lax.all_to_all(d_kv, "mp", 0, 0, axis_index_groups=y_groups, tiled=True)
    (weight_parts,) = call(
        weight_grad_kernel,
        "weight_grads",
        [((2 * HELD, 2 * HEAD_DIM, width // 2), BF16)],
        (attended, d_queries, hidden, upstream),
    )
    weight_parts, d_kv_got = lax.optimization_barrier((weight_parts, d_kv_got))

    weight_got = lax.all_to_all(weight_parts, both, 0, 0, axis_index_groups=yx_groups, tiled=True)
    rows = 2 * CAP + FRAMES
    send_x, send_own, keep = call(
        update_kernel,
        "updates",
        [((rows, width), BF16), ((rows, width), BF16), ((2, rows, width), BF16)],
        (meta, d_kv_got, attended, d_queries, kv_got, qo_got),
        mib=24,
        scratch=[pltpu.VMEM((HELD * FRAMES, WIDTH), BF16), pltpu.VMEM((HELD * FRAMES, WIDTH), BF16)],
        scalars=1,
    )
    core_x = lax.ppermute(send_x, "mp", swap_core)
    core_own = lax.ppermute(send_own, "mp", swap_core)
    (x_out,) = call(add_kernel, "add_updates", [((rows, width), BF16)], ((keep, 1), core_x), mib=8)
    x_parts = lax.ppermute(x_out, "mp", swap_x)
    weight_got, _ = lax.optimization_barrier((weight_got, x_out))

    (weight_half,) = call(
        grad_sum_kernel, "sum_weight_grads", [((width // 2, 2 * HEAD_DIM), BF16)], (weight_got,), mib=8
    )
    weight_last = lax.all_to_all(
        weight_half.reshape(depth, width // (2 * depth), 2 * HEAD_DIM),
        both,
        0,
        0,
        axis_index_groups=z_groups,
        tiled=True,
    )
    x_parts, _ = lax.optimization_barrier((x_parts, weight_half))
    cross_update, grad_captions, grad_audio = call(
        final_kernel,
        "final_rows",
        [((CAP, width), BF16), ((CAP, width), BF16), ((1, FRAMES, width), BF16)],
        ((keep, 0), core_own, x_parts, captions, dec_gain, audio, enc_gain),
        mib=16,
    )
    weight_last, cross_update, grad_captions, grad_audio = lax.optimization_barrier(
        (weight_last, cross_update, grad_captions, grad_audio)
    )
    rows = width // (2 * depth)
    grad_wq, grad_wo = pl.pallas_call(
        grad_final_kernel,
        out_shape=(jax.ShapeDtypeStruct((rows, HEAD_DIM), F32),) * 2,
        compiler_params=params(16),
        name="final_weight_grads",
    )(weight_last)
    return (cross_update, grad_captions, grad_audio, grad_wq, grad_wo.T)


def device_groups(dp_size):
    depth = dp_size // 2

    def device(x_hi, z, x_lo, y, core):
        return (x_hi * depth + z) * 16 + (x_lo * 4 + y) * 2 + core

    y_groups = [[(x * 4 + y) * 2 + core for y in range(4)] for x in range(2) for core in range(2)]
    yx_groups = [
        [device(x_hi, z, x_lo, y, core) for x_hi in range(2) for y in range(4)]
        for z in range(depth)
        for x_lo in range(2)
        for core in range(2)
    ]
    z_groups = [
        [device(x_hi, z, x_lo, y, core) for z in range(depth)]
        for x_hi in range(2)
        for x_lo in range(2)
        for y in range(4)
        for core in range(2)
    ]
    return dict(depth=depth, y_groups=y_groups, yx_groups=yx_groups, z_groups=z_groups)


def solution(mesh):
    in_specs = (
        P(("dp", "mp"), None),
        P(("dp", "mp"), None, None),
        P("dp"),
        P("dp", None),
        P(),
        P(),
        P(),
        P(),
        P(None, "mp"),
        P(None, "mp"),
        P(None, "mp"),
        P("mp", None),
        P(("dp", "mp"), None),
    )
    out_specs = (
        P(("dp", "mp"), None),
        P(("dp", "mp"), None),
        P(("dp", "mp"), None, None),
        P("dp", "mp"),
        P("mp", "dp"),
    )
    local = functools.partial(body, **device_groups(mesh.shape["dp"]))
    return jax.shard_map(local, mesh=mesh, in_specs=in_specs, out_specs=out_specs, check_vma=False)
```

```python
import functools
import math

import jax
import jax.numpy as jnp
from jax import lax
from jax.experimental import pallas as pl
from jax.experimental.pallas import tpu as pltpu
from jax.sharding import PartitionSpec as P

HEAD_DIM = 64
EPSILON = 1e-05
FRAMES = 32
CAP = 128
HELD = 4
ROWS = HELD * CAP
WIDTH = HELD * HEAD_DIM
BF16 = jnp.bfloat16
F32 = jnp.float32
LARGEST_BF16 = 3.3895313892515355e38

HBM = pl.BlockSpec(memory_space=pltpu.HBM)
MIB = 1 << 20
BIG = 60
COST = pl.CostEstimate(flops=1000, bytes_accessed=1000, transcendentals=0)


def params(mib):
    return pltpu.CompilerParams(vmem_limit_bytes=mib * MIB)


def dot(left, right, left_dim=1, right_dim=0):
    return lax.dot_general(
        left, right, (((left_dim,), (right_dim,)), ((), ())), preferred_element_type=F32
    )


def standardize(values):
    row_mean = jnp.mean(values, axis=-1, keepdims=True)
    centred = values - row_mean
    inverse_std = lax.rsqrt(jnp.mean(centred * centred, axis=-1, keepdims=True) + EPSILON)
    return centred * inverse_std, inverse_std


def norm_backward(upstream, normed, inverse_std, gain_vec):
    scaled = upstream * gain_vec
    mean_term = jnp.mean(scaled, axis=-1, keepdims=True)
    cross_term = jnp.mean(scaled * normed, axis=-1, keepdims=True)
    return inverse_std * (scaled - mean_term - normed * cross_term)


def held_caption(own, part):
    return own ^ ((part & 1) * 8) ^ (part >> 1)


def caption_length(meta, caption):
    return meta[1 + caption]


def described_clip(meta, caption):
    return meta[17 + caption]


def row_of_y(own):
    return (own >> 1) & 3


def weight_of(w_ref, kind):
    rows = w_ref[:, kind * HEAD_DIM : (kind + 1) * HEAD_DIM, :]
    return rows.reshape(WIDTH, w_ref.shape[2])


def pack_kernel(*refs):
    count = len(refs) // 2 - 1
    blocks, out_ref, held, sems = refs[:count], refs[count], refs[count + 1 : -1], refs[-1]
    copies = [pltpu.make_async_copy(block, here, sems.at[k, HELD]) for k, (block, here) in enumerate(zip(blocks, held))]
    for copy in copies:
        copy.start()
    sent, first = [], 0
    for k, here in enumerate(held):
        copies[k].wait()
        for target in range(HELD):
            place = out_ref.at[target, pl.ds(first, here.shape[0])]
            sent.append(pltpu.make_async_copy(here, place, sems.at[k, target]))
            sent[-1].start()
        first += here.shape[0]
    for copy in sent:
        copy.wait()


def pack(name, *blocks):
    rows = sum(block.shape[0] for block in blocks)
    return pl.pallas_call(
        pack_kernel,
        out_shape=jax.ShapeDtypeStruct((HELD, rows, blocks[0].shape[1]), BF16),
        in_specs=[HBM] * len(blocks),
        out_specs=HBM,
        scratch_shapes=[pltpu.VMEM(block.shape, BF16) for block in blocks]
        + [pltpu.SemaphoreType.DMA((len(blocks), HELD + 1))],
        compiler_params=params(BIG),
        cost_estimate=COST,
        name=name,
    )(*blocks)


def norm_kernel(first, io, meta, t0, t1, gain, bias, hid_ref, up_ref):
    width = hid_ref.shape[1]
    io.take(0, 3, 4)
    own = meta[0]
    positions = lax.broadcasted_iota(jnp.int32, (CAP, 1), 0)
    gain_row, bias_row = gain[...].reshape(1, width), bias[...].reshape(1, width)
    for place, tokens in enumerate((t0, t1)):
        io.take(1 + place)
        span = slice(place * CAP, (place + 1) * CAP)
        normed, _ = standardize(tokens[0].astype(F32))
        hid_ref[span, :] = (normed * gain_row + bias_row).astype(BF16)
        live = positions < caption_length(meta, held_caption(own, first + 2 * place))
        up_ref[span, :] = jnp.where(live, tokens[1].astype(F32), 0.0).astype(BF16)


def segment_sum(values, ones):
    high = jnp.minimum(values, LARGEST_BF16).astype(BF16)
    low = (values - high.astype(F32)).astype(BF16)
    return dot(high, ones) + dot(low, ones)


def key_value_kernel(io, meta, gain, bias, kv_ref, near_ref, other_ref, out_ref, states_ref):
    width = states_ref.shape[1]
    io.take(0, 1, 2, 4, 5)
    own = meta[0]
    gain_row, bias_row = gain[...].reshape(1, width), bias[...].reshape(1, width)
    for part in range(HELD):
        clip = described_clip(meta, held_caption(own, part))
        place = row_of_y(clip) + 4 * ((clip ^ own) >> 3)
        near = ((clip ^ own) & 1) == 0
        frames = jnp.where(near, near_ref[place].astype(F32), other_ref[place].astype(F32))
        normed, _ = standardize(frames)
        states_ref[part * FRAMES : (part + 1) * FRAMES, :] = (normed * gain_row + bias_row).astype(BF16)
    io.take(3)
    for kind in range(2):
        out_ref[kind] = dot(states_ref[...], weight_of(kv_ref, kind), 1, 1).astype(BF16)


def join(target, near, far):
    for place in range(2):
        rows = slice(place * CAP, (place + 1) * CAP)
        target[2 * place * CAP : (2 * place + 1) * CAP, :] = near[rows, :]
        target[(2 * place + 1) * CAP : (2 * place + 2) * CAP, :] = far[rows, :]


def attend_kernel(io, kv_ref, qo_ref, h0, u0, h1, u1, dkv_ref, rows_ref, hid_ref, up_ref):
    scale = 1.0 / math.sqrt(HEAD_DIM)
    pairs = HELD * FRAMES
    row_head = lax.broadcasted_iota(jnp.int32, (pairs, WIDTH), 0) // FRAMES
    lane_head = lax.broadcasted_iota(jnp.int32, (pairs, WIDTH), 1) // HEAD_DIM
    same = row_head == lane_head
    first = lax.broadcasted_iota(jnp.int32, (pairs, pairs), 0) // FRAMES
    second = lax.broadcasted_iota(jnp.int32, (pairs, pairs), 1) // FRAMES
    ones = jnp.where(first == second, 1.0, 0.0).astype(BF16)
    parts = range(HELD)
    spans = [slice(part * CAP, (part + 1) * CAP) for part in parts]

    def spread(rows):
        repeated = jnp.concatenate([rows.astype(F32)] * HELD, axis=0)
        return jnp.where(same, repeated, 0.0).astype(BF16)

    def collect(rows):
        kept = jnp.where(same, rows, 0.0)
        total = kept[0:FRAMES]
        for head in range(1, HELD):
            total = total + kept[head * FRAMES : (head + 1) * FRAMES]
        return total.astype(BF16)

    io.take(0)
    blocks = [[spread(kv_ref[kind, part * FRAMES : (part + 1) * FRAMES]) for part in parts] for kind in range(2)]
    keys, values = blocks
    io.take(1, 2, 4)
    join(hid_ref, h0, h1)
    queries = dot(hid_ref[...], weight_of(qo_ref, 0), 1, 1).astype(BF16)
    query = [queries[span] for span in spans]
    io.take(3, 5)
    join(up_ref, u0, u1)
    d_attended = dot(up_ref[...], weight_of(qo_ref, 1), 1, 1).astype(BF16)
    d_att = [d_attended[span] for span in spans]
    weights = [jnp.exp(dot(query[part], keys[part], 1, 1) * scale) for part in parts]
    d_softmax = [dot(d_att[part], values[part], 1, 1) for part in parts]
    sums = [segment_sum(weights[part], ones) for part in parts]
    softmax = [weights[part] / sums[part] for part in parts]
    low = [softmax[part].astype(BF16) for part in parts]
    inner = [segment_sum(softmax[part] * d_softmax[part], ones) for part in parts]
    d_values = [dot(low[part], d_att[part], 0, 0) for part in parts]
    d_scores = [(softmax[part] * (d_softmax[part] - inner[part]) * scale).astype(BF16) for part in parts]
    d_keys = [dot(d_scores[part], query[part], 0, 0) for part in parts]
    for kind, found in enumerate((d_keys, d_values)):
        for part in parts:
            block = collect(found[part])
            for row in range(HELD):
                dkv_ref[row, kind, part] = block
    io.give(0)
    for part in parts:
        rows_ref[0, spans[part], :] = dot(low[part], values[part]).astype(BF16)
        rows_ref[1, spans[part], :] = dot(d_scores[part], keys[part]).astype(BF16)


def product_kernel(
    io, rows_ref, h0, u0, h1, u1, qo_ref, grad_ref, send_x, send_own, keep_ref, hid_ref, up_ref
):
    io.take(0, 1, 2, 3, 4)
    join(hid_ref, h0, h1)
    join(up_ref, u0, u1)
    half = hid_ref.shape[1] // 2
    for kind, right in enumerate((hid_ref, up_ref)):
        for side in range(2):
            product = dot(rows_ref[1 - kind], right[:, side * half : (side + 1) * half], 0, 0).astype(BF16)
            for head in range(HELD):
                grad_ref[side * HELD + head, kind * HEAD_DIM : (kind + 1) * HEAD_DIM, :] = product[
                    head * HEAD_DIM : (head + 1) * HEAD_DIM
                ]
    io.give(0)
    io.take(5)
    w_query, w_out = weight_of(qo_ref, 0), weight_of(qo_ref, 1)
    for part in range(HELD):
        target = (keep_ref.at[0], keep_ref.at[1], send_own, send_x)[part]
        span = slice(part * CAP, (part + 1) * CAP)
        target[:CAP, :] = dot(rows_ref[0, span], w_out).astype(BF16)
        target[CAP : 2 * CAP, :] = dot(rows_ref[1, span], w_query).astype(BF16)
        target[2 * CAP :, :] = jnp.zeros((FRAMES, target.shape[1]), BF16)


def state_kernel(
    meta_in, got_in, kv_in, x_in, own_in, keep_in, x_out, own_out, keep_out, meta, got_ref, kv_ref, made, sems, keys_ref, values_ref
):
    del x_in, own_in, keep_in
    copies = [
        pltpu.make_async_copy(source, target, sems.at[place])
        for place, (source, target) in enumerate(((meta_in, meta), (got_in, got_ref), (kv_in, kv_ref)))
    ]
    for copy in copies:
        copy.start()
    for copy in copies:
        copy.wait()
    own = meta[0]
    for part in range(HELD):
        clip = held_caption(own, part)
        caption = 0
        for index in range(4 * HELD):
            caption = jnp.where(described_clip(meta, index) == clip, index, caption)
        row = row_of_y(caption)
        apart = caption ^ own
        place = (apart >> 3) + 2 * (apart & 1)
        keys_ref[part * FRAMES : (part + 1) * FRAMES, :] = got_ref[row, 0, place]
        values_ref[part * FRAMES : (part + 1) * FRAMES, :] = got_ref[row, 1, place]
    total = dot(keys_ref[...], weight_of(kv_ref, 0)) + dot(values_ref[...], weight_of(kv_ref, 1))
    copies = []
    for part in range(HELD):
        made[part] = total[part * FRAMES : (part + 1) * FRAMES].astype(BF16)
        target = (keep_out.at[0], keep_out.at[1], own_out, x_out)[part]
        copies.append(
            pltpu.make_async_copy(made.at[part], target.at[pl.ds(2 * CAP, FRAMES)], sems.at[3 + part])
        )
        copies[-1].start()
    for copy in copies:
        copy.wait()


def grad_sum_kernel(io, parts_ref, out_ref):
    io.take()
    total = parts_ref[0].astype(F32)
    for part in range(1, parts_ref.shape[0]):
        total = total + parts_ref[part].astype(F32)
    out_ref[...] = total.T.astype(BF16)


def grad_final_kernel(parts_ref, wq_ref, wo_ref):
    total = parts_ref[0].astype(F32)
    for part in range(1, parts_ref.shape[0]):
        total = total + parts_ref[part].astype(F32)
    wq_ref[...] = total[:, :HEAD_DIM]
    wo_ref[...] = total[:, HEAD_DIM:]


def add_kernel(io, left_ref, right_ref, out_ref):
    io.take()
    out_ref[...] = (left_ref[...].astype(F32) + right_ref[...].astype(F32)).astype(BF16)


def final_kernel(
    io, keep_ref, core_ref, x_ref, caption_ref, dec_gain, audio_ref, enc_gain, update_ref, grad_ref, out_ref
):
    io.take()
    width = caption_ref.shape[1]

    def total(start, stop):
        near = keep_ref[start:stop].astype(F32) + core_ref[start:stop].astype(F32)
        return near + x_ref[start:stop].astype(F32)

    update_ref[...] = total(0, CAP).astype(BF16)
    io.give(0)
    normed, inverse_std = standardize(caption_ref[...].astype(F32))
    d_hidden = total(CAP, 2 * CAP)
    grad_ref[...] = norm_backward(d_hidden, normed, inverse_std, dec_gain[...].reshape(1, width)).astype(BF16)
    io.give(1)
    normed, inverse_std = standardize(audio_ref[0].astype(F32))
    d_states = total(2 * CAP, 2 * CAP + FRAMES)
    out_ref[0] = norm_backward(d_states, normed, inverse_std, enc_gain[...].reshape(1, width)).astype(BF16)


class Transfers:
    def __init__(self, takes, gives):
        self.takes, self.gives = dict(enumerate(takes)), dict(enumerate(gives))
        self.given = []
        for copy in takes:
            copy.start()

    def take(self, *places):
        for place in places or tuple(self.takes):
            self.takes.pop(place).wait()

    def give(self, *places):
        for place in places or tuple(self.gives):
            self.given.append(self.gives.pop(place))
            self.given[-1].start()

    def finish(self):
        if self.gives:
            self.give()
        for copy in self.given:
            copy.wait()


def call(kernel, name, outs, operands, mib=BIG, scratch=(), scalars=0):
    takes, gives = len(operands), len(outs)
    places = [operand[1] if isinstance(operand, tuple) else None for operand in operands]
    operands = [operand[0] if isinstance(operand, tuple) else operand for operand in operands]

    def copied(*refs):
        given, wanted, refs = refs[:takes], refs[takes : takes + gives], refs[takes + gives :]
        held, made, refs = refs[:takes], refs[takes : takes + gives], refs[takes + gives :]
        sems, rest = refs[0], refs[1:]
        io = Transfers(
            [
                pltpu.make_async_copy(
                    given[i] if places[i] is None else given[i].at[places[i]], held[i], sems.at[i]
                )
                for i in range(takes)
            ],
            [pltpu.make_async_copy(made[i], wanted[i], sems.at[takes + i]) for i in range(gives)],
        )
        kernel(io, *held, *made, *rest)
        io.finish()

    def space(place, array):
        shape = array.shape if places[place] is None else array.shape[1:]
        return (pltpu.SMEM if place < scalars else pltpu.VMEM)(shape, array.dtype)

    return pl.pallas_call(
        copied,
        out_shape=tuple(jax.ShapeDtypeStruct(*out) for out in outs),
        in_specs=[HBM] * takes,
        out_specs=(HBM,) * gives,
        scratch_shapes=[space(place, operand) for place, operand in enumerate(operands)]
        + [pltpu.VMEM(*out) for out in outs]
        + [pltpu.SemaphoreType.DMA((takes + gives,))]
        + list(scratch),
        compiler_params=params(mib),
        cost_estimate=COST,
        name=name,
    )(*operands)


def body(
    captions,
    audio,
    caption_len,
    pairing,
    enc_gain,
    enc_bias,
    dec_gain,
    dec_bias,
    w_query,
    w_key,
    w_value,
    w_out,
    grad_update,
    *,
    depth,
    y_groups,
    yx_groups,
    z_groups,
):
    both = ("dp", "mp")
    width = captions.shape[1]
    own = lax.axis_index("mp").astype(jnp.int32).reshape(1)
    meta = jnp.concatenate([own, caption_len, pairing[0], jnp.zeros((95,), jnp.int32)])
    swap_core = [(index, index ^ 1) for index in range(16)]
    swap_x = [(index, index ^ 8) for index in range(16)]

    kv_out = pack("pack_keys_values", w_key.T, w_value.T, audio.reshape(FRAMES, width))
    kv_got = lax.all_to_all(kv_out, "mp", 0, 0, axis_index_groups=y_groups, tiled=True)
    qo_out = pack("pack_queries_out", w_query.T, w_out)
    tokens_own = jnp.stack([captions, grad_update])
    tokens_x = lax.ppermute(tokens_own, "mp", swap_x)
    tokens_core = lax.ppermute(tokens_own, "mp", swap_core)

    def norms(first, name, near, other):
        return call(
            functools.partial(norm_kernel, first),
            name,
            [((2 * CAP, width), BF16), ((2 * CAP, width), BF16)],
            (meta, near, other, dec_gain, dec_bias),
            scalars=1,
        )

    normed_near = norms(0, "norms_near", tokens_own, tokens_core)
    kv_got, qo_out, *normed_near = lax.optimization_barrier((kv_got, qo_out, *normed_near))
    qo_got = lax.all_to_all(qo_out, "mp", 0, 0, axis_index_groups=y_groups, tiled=True)
    audio_y = kv_got[:, 2 * HEAD_DIM :]
    audio_near = jnp.concatenate([audio_y, lax.ppermute(audio_y, "mp", swap_x)])
    audio_other = lax.ppermute(audio_near, "mp", swap_core)
    (keys_values,) = call(
        key_value_kernel,
        "keys_values",
        [((2, HELD * FRAMES, WIDTH), BF16)],
        (meta, enc_gain, enc_bias, kv_got, audio_near, audio_other),
        scratch=[pltpu.VMEM((HELD * FRAMES, width), BF16)],
        scalars=1,
    )
    tokens_far = lax.ppermute(tokens_x, "mp", swap_core)
    normed_far = norms(1, "norms_far", tokens_x, tokens_far)

    d_kv, attended = call(
        attend_kernel,
        "attend",
        [((HELD, 2, HELD, FRAMES, WIDTH), BF16), ((2, ROWS, WIDTH), BF16)],
        (keys_values, qo_got, *normed_near, *normed_far),
        scratch=[pltpu.VMEM((ROWS, width), BF16)] * 2,
    )
    d_kv_got = lax.all_to_all(d_kv, "mp", 0, 0, axis_index_groups=y_groups, tiled=True)
    rows = 2 * CAP + FRAMES
    weight_parts, send_x, send_own, keep = call(
        product_kernel,
        "products",
        [
            ((2 * HELD, 2 * HEAD_DIM, width // 2), BF16),
            ((rows, width), BF16),
            ((rows, width), BF16),
            ((2, rows, width), BF16),
        ],
        (attended, *normed_near, *normed_far, qo_got),
        scratch=[pltpu.VMEM((ROWS, width), BF16)] * 2,
    )
    d_kv_got, weight_parts = lax.optimization_barrier((d_kv_got, weight_parts))
    weight_got = lax.all_to_all(weight_parts, both, 0, 0, axis_index_groups=yx_groups, tiled=True)
    send_x, send_own, keep = pl.pallas_call(
        state_kernel,
        out_shape=tuple(jax.ShapeDtypeStruct(array.shape, BF16) for array in (send_x, send_own, keep)),
        in_specs=[HBM] * 6,
        out_specs=(HBM,) * 3,
        input_output_aliases={3: 0, 4: 1, 5: 2},
        scratch_shapes=[
            pltpu.SMEM(meta.shape, meta.dtype),
            pltpu.VMEM(d_kv_got.shape, BF16),
            pltpu.VMEM(kv_got.shape, BF16),
            pltpu.VMEM((HELD, FRAMES, width), BF16),
            pltpu.SemaphoreType.DMA((3 + HELD,)),
        ]
        + [pltpu.VMEM((HELD * FRAMES, WIDTH), BF16)] * 2,
        compiler_params=params(BIG),
        cost_estimate=COST,
        name="state_grads",
    )(meta, d_kv_got, kv_got, send_x, send_own, keep)
    core_x = lax.ppermute(send_x, "mp", swap_core)
    core_own = lax.ppermute(send_own, "mp", swap_core)
    (x_out,) = call(add_kernel, "add_updates", [((rows, width), BF16)], ((keep, 1), core_x), mib=8)
    x_parts = lax.ppermute(x_out, "mp", swap_x)
    weight_got, _ = lax.optimization_barrier((weight_got, x_out))

    (weight_half,) = call(
        grad_sum_kernel, "sum_weight_grads", [((width // 2, 2 * HEAD_DIM), BF16)], (weight_got,), mib=8
    )
    weight_last = lax.all_to_all(
        weight_half.reshape(depth, width // (2 * depth), 2 * HEAD_DIM),
        both,
        0,
        0,
        axis_index_groups=z_groups,
        tiled=True,
    )
    x_parts, _ = lax.optimization_barrier((x_parts, weight_half))
    cross_update, grad_captions, grad_audio = call(
        final_kernel,
        "final_rows",
        [((CAP, width), BF16), ((CAP, width), BF16), ((1, FRAMES, width), BF16)],
        ((keep, 0), core_own, x_parts, captions, dec_gain, audio, enc_gain),
        mib=16,
    )
    weight_last, cross_update, grad_captions, grad_audio = lax.optimization_barrier(
        (weight_last, cross_update, grad_captions, grad_audio)
    )
    rows = width // (2 * depth)
    grad_wq, grad_wo = pl.pallas_call(
        grad_final_kernel,
        out_shape=(jax.ShapeDtypeStruct((rows, HEAD_DIM), F32),) * 2,
        compiler_params=params(16),
        name="final_weight_grads",
    )(weight_last)
    return (cross_update, grad_captions, grad_audio, grad_wq, grad_wo.T)


def device_groups(dp_size):
    depth = dp_size // 2

    def device(x_hi, z, x_lo, y, core):
        return (x_hi * depth + z) * 16 + (x_lo * 4 + y) * 2 + core

    y_groups = [[(x * 4 + y) * 2 + core for y in range(4)] for x in range(2) for core in range(2)]
    yx_groups = [
        [device(x_hi, z, x_lo, y, core) for x_hi in range(2) for y in range(4)]
        for z in range(depth)
        for x_lo in range(2)
        for core in range(2)
    ]
    z_groups = [
        [device(x_hi, z, x_lo, y, core) for z in range(depth)]
        for x_hi in range(2)
        for x_lo in range(2)
        for y in range(4)
        for core in range(2)
    ]
    return dict(depth=depth, y_groups=y_groups, yx_groups=yx_groups, z_groups=z_groups)


def solution(mesh):
    in_specs = (
        P(("dp", "mp"), None),
        P(("dp", "mp"), None, None),
        P("dp"),
        P("dp", None),
        P(),
        P(),
        P(),
        P(),
        P(None, "mp"),
        P(None, "mp"),
        P(None, "mp"),
        P("mp", None),
        P(("dp", "mp"), None),
    )
    out_specs = (
        P(("dp", "mp"), None),
        P(("dp", "mp"), None),
        P(("dp", "mp"), None, None),
        P("dp", "mp"),
        P("mp", "dp"),
    )
    local = functools.partial(body, **device_groups(mesh.shape["dp"]))
    return jax.shard_map(local, mesh=mesh, in_specs=in_specs, out_specs=out_specs, check_vma=False)
```

```python
import functools
import math

import jax
import jax.numpy as jnp
from jax import lax
from jax.experimental import pallas as pl
from jax.experimental.pallas import tpu as pltpu
from jax.sharding import PartitionSpec as P

HEAD_DIM = 64
EPSILON = 1e-05
FRAMES = 32
CAP = 128
HELD = 4
ROWS = HELD * CAP
WIDTH = HELD * HEAD_DIM
BF16 = jnp.bfloat16
F32 = jnp.float32
LARGEST_BF16 = 3.3895313892515355e38

HBM = pl.BlockSpec(memory_space=pltpu.HBM)
MIB = 1 << 20
BIG = 60
COST = pl.CostEstimate(flops=1000, bytes_accessed=1000, transcendentals=0)


def params(mib):
    return pltpu.CompilerParams(vmem_limit_bytes=mib * MIB)


def dot(left, right, left_dim=1, right_dim=0):
    return lax.dot_general(
        left, right, (((left_dim,), (right_dim,)), ((), ())), preferred_element_type=F32
    )


def standardize(values):
    row_mean = jnp.mean(values, axis=-1, keepdims=True)
    centred = values - row_mean
    inverse_std = lax.rsqrt(jnp.mean(centred * centred, axis=-1, keepdims=True) + EPSILON)
    return centred * inverse_std, inverse_std


def norm_backward(upstream, normed, inverse_std, gain_vec):
    scaled = upstream * gain_vec
    mean_term = jnp.mean(scaled, axis=-1, keepdims=True)
    cross_term = jnp.mean(scaled * normed, axis=-1, keepdims=True)
    return inverse_std * (scaled - mean_term - normed * cross_term)


def held_caption(own, part):
    return own ^ ((part & 1) * 8) ^ (part >> 1)


def caption_length(meta, caption):
    return meta[1 + caption]


def described_clip(meta, caption):
    return meta[17 + caption]


def row_of_y(own):
    return (own >> 1) & 3


def weight_of(w_ref, kind):
    rows = w_ref[:, kind * HEAD_DIM : (kind + 1) * HEAD_DIM, :]
    return rows.reshape(WIDTH, w_ref.shape[2])


def pack_kernel(*refs):
    count = len(refs) // 2 - 1
    blocks, out_ref, held, sems = refs[:count], refs[count], refs[count + 1 : -1], refs[-1]
    copies = [pltpu.make_async_copy(block, here, sems.at[k, HELD]) for k, (block, here) in enumerate(zip(blocks, held))]
    for copy in copies:
        copy.start()
    sent, first = [], 0
    for k, here in enumerate(held):
        copies[k].wait()
        for target in range(HELD):
            place = out_ref.at[target, pl.ds(first, here.shape[0])]
            sent.append(pltpu.make_async_copy(here, place, sems.at[k, target]))
            sent[-1].start()
        first += here.shape[0]
    for copy in sent:
        copy.wait()


def pack(name, *blocks):
    rows = sum(block.shape[0] for block in blocks)
    return pl.pallas_call(
        pack_kernel,
        out_shape=jax.ShapeDtypeStruct((HELD, rows, blocks[0].shape[1]), BF16),
        in_specs=[HBM] * len(blocks),
        out_specs=HBM,
        scratch_shapes=[pltpu.VMEM(block.shape, BF16) for block in blocks]
        + [pltpu.SemaphoreType.DMA((len(blocks), HELD + 1))],
        compiler_params=params(BIG),
        cost_estimate=COST,
        name=name,
    )(*blocks)


def norm_kernel(first, io, meta, t0, t1, gain, bias, hid_ref, up_ref):
    width = hid_ref.shape[1]
    io.take(0, 3, 4)
    own = meta[0]
    positions = lax.broadcasted_iota(jnp.int32, (CAP, 1), 0)
    gain_row, bias_row = gain[...].reshape(1, width), bias[...].reshape(1, width)
    for place, tokens in enumerate((t0, t1)):
        io.take(1 + place)
        span = slice(place * CAP, (place + 1) * CAP)
        normed, _ = standardize(tokens[0].astype(F32))
        hid_ref[span, :] = (normed * gain_row + bias_row).astype(BF16)
        live = positions < caption_length(meta, held_caption(own, first + 2 * place))
        up_ref[span, :] = jnp.where(live, tokens[1].astype(F32), 0.0).astype(BF16)


def segment_sum(values, ones):
    high = jnp.minimum(values, LARGEST_BF16).astype(BF16)
    low = (values - high.astype(F32)).astype(BF16)
    return dot(high, ones) + dot(low, ones)


def key_value_kernel(io, meta, gain, bias, kv_ref, near_ref, other_ref, out_ref, states_ref):
    width = states_ref.shape[1]
    io.take(0, 1, 2, 4, 5)
    own = meta[0]
    gain_row, bias_row = gain[...].reshape(1, width), bias[...].reshape(1, width)
    for part in range(HELD):
        clip = described_clip(meta, held_caption(own, part))
        place = row_of_y(clip) + 4 * ((clip ^ own) >> 3)
        near = ((clip ^ own) & 1) == 0
        frames = jnp.where(near, near_ref[place].astype(F32), other_ref[place].astype(F32))
        normed, _ = standardize(frames)
        states_ref[part * FRAMES : (part + 1) * FRAMES, :] = (normed * gain_row + bias_row).astype(BF16)
    io.take(3)
    for kind in range(2):
        out_ref[kind] = dot(states_ref[...], weight_of(kv_ref, kind), 1, 1).astype(BF16)


def join(target, near, far):
    for place in range(2):
        rows = slice(place * CAP, (place + 1) * CAP)
        target[2 * place * CAP : (2 * place + 1) * CAP, :] = near[rows, :]
        target[(2 * place + 1) * CAP : (2 * place + 2) * CAP, :] = far[rows, :]


def attend_kernel(io, kv_ref, qo_ref, h0, u0, h1, u1, dkv_ref, rows_ref, hid_ref, up_ref):
    scale = 1.0 / math.sqrt(HEAD_DIM)
    pairs = HELD * FRAMES
    row_head = lax.broadcasted_iota(jnp.int32, (pairs, WIDTH), 0) // FRAMES
    lane_head = lax.broadcasted_iota(jnp.int32, (pairs, WIDTH), 1) // HEAD_DIM
    same = row_head == lane_head
    first = lax.broadcasted_iota(jnp.int32, (pairs, pairs), 0) // FRAMES
    second = lax.broadcasted_iota(jnp.int32, (pairs, pairs), 1) // FRAMES
    ones = jnp.where(first == second, 1.0, 0.0).astype(BF16)
    parts = range(HELD)
    spans = [slice(part * CAP, (part + 1) * CAP) for part in parts]

    def spread(rows):
        repeated = jnp.concatenate([rows.astype(F32)] * HELD, axis=0)
        return jnp.where(same, repeated, 0.0).astype(BF16)

    def collect(rows):
        kept = jnp.where(same, rows, 0.0)
        total = kept[0:FRAMES]
        for head in range(1, HELD):
            total = total + kept[head * FRAMES : (head + 1) * FRAMES]
        return total.astype(BF16)

    io.take(0)
    blocks = [[spread(kv_ref[kind, part * FRAMES : (part + 1) * FRAMES]) for part in parts] for kind in range(2)]
    keys, values = blocks
    io.take(1, 2, 4)
    join(hid_ref, h0, h1)
    queries = dot(hid_ref[...], weight_of(qo_ref, 0), 1, 1).astype(BF16)
    query = [queries[span] for span in spans]
    io.take(3, 5)
    join(up_ref, u0, u1)
    d_attended = dot(up_ref[...], weight_of(qo_ref, 1), 1, 1).astype(BF16)
    d_att = [d_attended[span] for span in spans]
    weights = [jnp.exp(dot(query[part], keys[part], 1, 1) * scale) for part in parts]
    d_softmax = [dot(d_att[part], values[part], 1, 1) for part in parts]
    sums = [segment_sum(weights[part], ones) for part in parts]
    softmax = [weights[part] / sums[part] for part in parts]
    low = [softmax[part].astype(BF16) for part in parts]
    inner = [segment_sum(softmax[part] * d_softmax[part], ones) for part in parts]
    d_values = [dot(low[part], d_att[part], 0, 0) for part in parts]
    d_scores = [(softmax[part] * (d_softmax[part] - inner[part]) * scale).astype(BF16) for part in parts]
    d_keys = [dot(d_scores[part], query[part], 0, 0) for part in parts]
    for kind, found in enumerate((d_keys, d_values)):
        for part in parts:
            block = collect(found[part])
            for row in range(HELD):
                dkv_ref[row, kind, part] = block
    io.give(0)
    for part in parts:
        rows_ref[0, spans[part], :] = dot(low[part], values[part]).astype(BF16)
        rows_ref[1, spans[part], :] = dot(d_scores[part], keys[part]).astype(BF16)


def product_kernel(
    io, rows_ref, h0, u0, h1, u1, qo_ref, grad_ref, send_x, send_update, send_rest, keep_ref, hid_ref, up_ref
):
    io.take(0, 1, 2, 3, 4)
    join(hid_ref, h0, h1)
    join(up_ref, u0, u1)
    half = hid_ref.shape[1] // 2
    for kind, right in enumerate((hid_ref, up_ref)):
        for side in range(2):
            product = dot(rows_ref[1 - kind], right[:, side * half : (side + 1) * half], 0, 0).astype(BF16)
            for head in range(HELD):
                grad_ref[side * HELD + head, kind * HEAD_DIM : (kind + 1) * HEAD_DIM, :] = product[
                    head * HEAD_DIM : (head + 1) * HEAD_DIM
                ]
    io.give(0)
    io.take(5)
    w_query, w_out = weight_of(qo_ref, 0), weight_of(qo_ref, 1)
    for part, (first, second) in enumerate(
        ((keep_ref.at[0], None), (keep_ref.at[1], None), (send_update, send_rest), (send_x, None))
    ):
        span = slice(part * CAP, (part + 1) * CAP)
        first[:CAP, :] = dot(rows_ref[0, span], w_out).astype(BF16)
        rest, start = (first, CAP) if second is None else (second, 0)
        rest[start : start + CAP, :] = dot(rows_ref[1, span], w_query).astype(BF16)
        rest[start + CAP :, :] = jnp.zeros((FRAMES, rest.shape[1]), BF16)


def state_kernel(meta_in, got_in, kv_in, *refs):
    send_x, send_rest, keep_ref, meta, got_ref, kv_ref, made, sems, keys_ref, values_ref = refs[3:]
    copies = [
        pltpu.make_async_copy(source, target, sems.at[place])
        for place, (source, target) in enumerate(((meta_in, meta), (got_in, got_ref), (kv_in, kv_ref)))
    ]
    for copy in copies:
        copy.start()
    for copy in copies:
        copy.wait()
    own = meta[0]
    for part in range(HELD):
        clip = held_caption(own, part)
        caption = 0
        for index in range(4 * HELD):
            caption = jnp.where(described_clip(meta, index) == clip, index, caption)
        row = row_of_y(caption)
        apart = caption ^ own
        place = (apart >> 3) + 2 * (apart & 1)
        keys_ref[part * FRAMES : (part + 1) * FRAMES, :] = got_ref[row, 0, place]
        values_ref[part * FRAMES : (part + 1) * FRAMES, :] = got_ref[row, 1, place]
    total = dot(keys_ref[...], weight_of(kv_ref, 0)) + dot(values_ref[...], weight_of(kv_ref, 1))
    copies = []
    for part in range(HELD):
        made[part] = total[part * FRAMES : (part + 1) * FRAMES].astype(BF16)
        target = (keep_ref.at[0], keep_ref.at[1], send_rest, send_x)[part]
        copies.append(
            pltpu.make_async_copy(made.at[part], target.at[pl.ds(target.shape[0] - FRAMES, FRAMES)], sems.at[3 + part])
        )
        copies[-1].start()
    for copy in copies:
        copy.wait()


def grad_sum_kernel(io, parts_ref, out_ref):
    io.take()
    total = parts_ref[0].astype(F32)
    for part in range(1, parts_ref.shape[0]):
        total = total + parts_ref[part].astype(F32)
    out_ref[...] = total.T.astype(BF16)


def grad_final_kernel(parts_ref, wq_ref, wo_ref):
    total = parts_ref[0].astype(F32)
    for part in range(1, parts_ref.shape[0]):
        total = total + parts_ref[part].astype(F32)
    wq_ref[...] = total[:, :HEAD_DIM]
    wo_ref[...] = total[:, HEAD_DIM:]


def add_kernel(io, left_ref, right_ref, out_ref):
    io.take()
    out_ref[...] = (left_ref[...].astype(F32) + right_ref[...].astype(F32)).astype(BF16)


def final_kernel(
    io,
    keep_ref,
    core_update,
    core_rest,
    x_ref,
    caption_ref,
    dec_gain,
    audio_ref,
    enc_gain,
    update_ref,
    grad_ref,
    out_ref,
):
    io.take()
    width = caption_ref.shape[1]

    def total(start, stop):
        core_ref, first = (core_update, 0) if start == 0 else (core_rest, CAP)
        near = keep_ref[start:stop].astype(F32) + core_ref[start - first : stop - first].astype(F32)
        return near + x_ref[start:stop].astype(F32)

    update_ref[...] = total(0, CAP).astype(BF16)
    io.give(0)
    normed, inverse_std = standardize(caption_ref[...].astype(F32))
    d_hidden = total(CAP, 2 * CAP)
    grad_ref[...] = norm_backward(d_hidden, normed, inverse_std, dec_gain[...].reshape(1, width)).astype(BF16)
    io.give(1)
    normed, inverse_std = standardize(audio_ref[0].astype(F32))
    d_states = total(2 * CAP, 2 * CAP + FRAMES)
    out_ref[0] = norm_backward(d_states, normed, inverse_std, enc_gain[...].reshape(1, width)).astype(BF16)


class Transfers:
    def __init__(self, takes, gives):
        self.takes, self.gives = dict(enumerate(takes)), dict(enumerate(gives))
        self.given = []
        for copy in takes:
            copy.start()

    def take(self, *places):
        for place in places or tuple(self.takes):
            self.takes.pop(place).wait()

    def give(self, *places):
        for place in places or tuple(self.gives):
            self.given.append(self.gives.pop(place))
            self.given[-1].start()

    def finish(self):
        if self.gives:
            self.give()
        for copy in self.given:
            copy.wait()


def call(kernel, name, outs, operands, mib=BIG, scratch=(), scalars=0):
    takes, gives = len(operands), len(outs)
    places = [operand[1] if isinstance(operand, tuple) else None for operand in operands]
    operands = [operand[0] if isinstance(operand, tuple) else operand for operand in operands]

    def copied(*refs):
        given, wanted, refs = refs[:takes], refs[takes : takes + gives], refs[takes + gives :]
        held, made, refs = refs[:takes], refs[takes : takes + gives], refs[takes + gives :]
        sems, rest = refs[0], refs[1:]
        io = Transfers(
            [
                pltpu.make_async_copy(
                    given[i] if places[i] is None else given[i].at[places[i]], held[i], sems.at[i]
                )
                for i in range(takes)
            ],
            [pltpu.make_async_copy(made[i], wanted[i], sems.at[takes + i]) for i in range(gives)],
        )
        kernel(io, *held, *made, *rest)
        io.finish()

    def space(place, array):
        shape = array.shape if places[place] is None else array.shape[1:]
        return (pltpu.SMEM if place < scalars else pltpu.VMEM)(shape, array.dtype)

    return pl.pallas_call(
        copied,
        out_shape=tuple(jax.ShapeDtypeStruct(*out) for out in outs),
        in_specs=[HBM] * takes,
        out_specs=(HBM,) * gives,
        scratch_shapes=[space(place, operand) for place, operand in enumerate(operands)]
        + [pltpu.VMEM(*out) for out in outs]
        + [pltpu.SemaphoreType.DMA((takes + gives,))]
        + list(scratch),
        compiler_params=params(mib),
        cost_estimate=COST,
        name=name,
    )(*operands)


def body(
    captions,
    audio,
    caption_len,
    pairing,
    enc_gain,
    enc_bias,
    dec_gain,
    dec_bias,
    w_query,
    w_key,
    w_value,
    w_out,
    grad_update,
    *,
    depth,
    y_groups,
    yx_groups,
    z_groups,
):
    both = ("dp", "mp")
    width = captions.shape[1]
    own = lax.axis_index("mp").astype(jnp.int32).reshape(1)
    meta = jnp.concatenate([own, caption_len, pairing[0], jnp.zeros((95,), jnp.int32)])
    swap_core = [(index, index ^ 1) for index in range(16)]
    swap_x = [(index, index ^ 8) for index in range(16)]

    kv_out = pack("pack_keys_values", w_key.T, w_value.T, audio.reshape(FRAMES, width))
    kv_got = lax.all_to_all(kv_out, "mp", 0, 0, axis_index_groups=y_groups, tiled=True)
    qo_out = pack("pack_queries_out", w_query.T, w_out)
    tokens_own = jnp.stack([captions, grad_update])
    tokens_x = lax.ppermute(tokens_own, "mp", swap_x)
    tokens_core = lax.ppermute(tokens_own, "mp", swap_core)

    def norms(first, name, near, other):
        return call(
            functools.partial(norm_kernel, first),
            name,
            [((2 * CAP, width), BF16), ((2 * CAP, width), BF16)],
            (meta, near, other, dec_gain, dec_bias),
            scalars=1,
        )

    normed_near = norms(0, "norms_near", tokens_own, tokens_core)
    kv_got, qo_out, *normed_near = lax.optimization_barrier((kv_got, qo_out, *normed_near))
    qo_got = lax.all_to_all(qo_out, "mp", 0, 0, axis_index_groups=y_groups, tiled=True)
    audio_y = kv_got[:, 2 * HEAD_DIM :]
    audio_near = jnp.concatenate([audio_y, lax.ppermute(audio_y, "mp", swap_x)])
    audio_other = lax.ppermute(audio_near, "mp", swap_core)
    (keys_values,) = call(
        key_value_kernel,
        "keys_values",
        [((2, HELD * FRAMES, WIDTH), BF16)],
        (meta, enc_gain, enc_bias, kv_got, audio_near, audio_other),
        scratch=[pltpu.VMEM((HELD * FRAMES, width), BF16)],
        scalars=1,
    )
    tokens_far = lax.ppermute(tokens_x, "mp", swap_core)
    normed_far = norms(1, "norms_far", tokens_x, tokens_far)

    d_kv, attended = call(
        attend_kernel,
        "attend",
        [((HELD, 2, HELD, FRAMES, WIDTH), BF16), ((2, ROWS, WIDTH), BF16)],
        (keys_values, qo_got, *normed_near, *normed_far),
        scratch=[pltpu.VMEM((ROWS, width), BF16)] * 2,
    )
    d_kv_got = lax.all_to_all(d_kv, "mp", 0, 0, axis_index_groups=y_groups, tiled=True)
    rows = 2 * CAP + FRAMES
    weight_parts, send_x, send_update, *partials = call(
        product_kernel,
        "products",
        [
            ((2 * HELD, 2 * HEAD_DIM, width // 2), BF16),
            ((rows, width), BF16),
            ((CAP, width), BF16),
            ((rows - CAP, width), BF16),
            ((2, rows, width), BF16),
        ],
        (attended, *normed_near, *normed_far, qo_got),
        scratch=[pltpu.VMEM((ROWS, width), BF16)] * 2,
    )
    d_kv_got, weight_parts = lax.optimization_barrier((d_kv_got, weight_parts))
    weight_got = lax.all_to_all(weight_parts, both, 0, 0, axis_index_groups=yx_groups, tiled=True)
    partials = (send_x, *partials)
    send_x, send_rest, keep = pl.pallas_call(
        state_kernel,
        out_shape=tuple(jax.ShapeDtypeStruct(array.shape, BF16) for array in partials),
        in_specs=[HBM] * 6,
        out_specs=(HBM,) * 3,
        input_output_aliases={3 + place: place for place in range(3)},
        scratch_shapes=[
            pltpu.SMEM(meta.shape, meta.dtype),
            pltpu.VMEM(d_kv_got.shape, BF16),
            pltpu.VMEM(kv_got.shape, BF16),
            pltpu.VMEM((HELD, FRAMES, width), BF16),
            pltpu.SemaphoreType.DMA((3 + HELD,)),
        ]
        + [pltpu.VMEM((HELD * FRAMES, WIDTH), BF16)] * 2,
        compiler_params=params(BIG),
        cost_estimate=COST,
        name="state_grads",
    )(meta, d_kv_got, kv_got, *partials)
    core_x = lax.ppermute(send_x, "mp", swap_core)
    (x_out,) = call(add_kernel, "add_updates", [((rows, width), BF16)], ((keep, 1), core_x), mib=8)
    x_parts = lax.ppermute(x_out, "mp", swap_x)
    weight_got, _ = lax.optimization_barrier((weight_got, x_out))

    (weight_half,) = call(
        grad_sum_kernel, "sum_weight_grads", [((width // 2, 2 * HEAD_DIM), BF16)], (weight_got,), mib=8
    )
    weight_last = lax.all_to_all(
        weight_half.reshape(depth, width // (2 * depth), 2 * HEAD_DIM),
        both,
        0,
        0,
        axis_index_groups=z_groups,
        tiled=True,
    )
    send_update, send_rest, _ = lax.optimization_barrier((send_update, send_rest, weight_half))
    core_update = lax.ppermute(send_update, "mp", swap_core)
    core_rest = lax.ppermute(send_rest, "mp", swap_core)
    cross_update, grad_captions, grad_audio = call(
        final_kernel,
        "final_rows",
        [((CAP, width), BF16), ((CAP, width), BF16), ((1, FRAMES, width), BF16)],
        ((keep, 0), core_update, core_rest, x_parts, captions, dec_gain, audio, enc_gain),
        mib=16,
    )
    weight_last, cross_update, grad_captions, grad_audio = lax.optimization_barrier(
        (weight_last, cross_update, grad_captions, grad_audio)
    )
    rows = width // (2 * depth)
    grad_wq, grad_wo = pl.pallas_call(
        grad_final_kernel,
        out_shape=(jax.ShapeDtypeStruct((rows, HEAD_DIM), F32),) * 2,
        compiler_params=params(16),
        name="final_weight_grads",
    )(weight_last)
    return (cross_update, grad_captions, grad_audio, grad_wq, grad_wo.T)


def device_groups(dp_size):
    depth = dp_size // 2

    def device(x_hi, z, x_lo, y, core):
        return (x_hi * depth + z) * 16 + (x_lo * 4 + y) * 2 + core

    y_groups = [[(x * 4 + y) * 2 + core for y in range(4)] for x in range(2) for core in range(2)]
    yx_groups = [
        [device(x_hi, z, x_lo, y, core) for x_hi in range(2) for y in range(4)]
        for z in range(depth)
        for x_lo in range(2)
        for core in range(2)
    ]
    z_groups = [
        [device(x_hi, z, x_lo, y, core) for z in range(depth)]
        for x_hi in range(2)
        for x_lo in range(2)
        for y in range(4)
        for core in range(2)
    ]
    return dict(depth=depth, y_groups=y_groups, yx_groups=yx_groups, z_groups=z_groups)


def solution(mesh):
    in_specs = (
        P(("dp", "mp"), None),
        P(("dp", "mp"), None, None),
        P("dp"),
        P("dp", None),
        P(),
        P(),
        P(),
        P(),
        P(None, "mp"),
        P(None, "mp"),
        P(None, "mp"),
        P("mp", None),
        P(("dp", "mp"), None),
    )
    out_specs = (
        P(("dp", "mp"), None),
        P(("dp", "mp"), None),
        P(("dp", "mp"), None, None),
        P("dp", "mp"),
        P("mp", "dp"),
    )
    local = functools.partial(body, **device_groups(mesh.shape["dp"]))
    return jax.shard_map(local, mesh=mesh, in_specs=in_specs, out_specs=out_specs, check_vma=False)
```

```python
import functools
import math

import jax
import jax.numpy as jnp
from jax import lax
from jax.experimental import pallas as pl
from jax.experimental.pallas import tpu as pltpu
from jax.sharding import PartitionSpec as P

HEAD_DIM = 64
EPSILON = 1e-05
FRAMES = 32
CAP = 128
HELD = 4
ROWS = HELD * CAP
WIDTH = HELD * HEAD_DIM
BF16 = jnp.bfloat16
F32 = jnp.float32
LARGEST_BF16 = 3.3895313892515355e38

HBM = pl.BlockSpec(memory_space=pltpu.HBM)
MIB = 1 << 20
BIG = 60
COST = pl.CostEstimate(flops=1000, bytes_accessed=1000, transcendentals=0)


def params(mib):
    return pltpu.CompilerParams(vmem_limit_bytes=mib * MIB)


def dot(left, right, left_dim=1, right_dim=0):
    return lax.dot_general(
        left, right, (((left_dim,), (right_dim,)), ((), ())), preferred_element_type=F32
    )


def standardize(values):
    row_mean = jnp.mean(values, axis=-1, keepdims=True)
    centred = values - row_mean
    inverse_std = lax.rsqrt(jnp.mean(centred * centred, axis=-1, keepdims=True) + EPSILON)
    return centred * inverse_std, inverse_std


def norm_backward(upstream, normed, inverse_std, gain_vec):
    scaled = upstream * gain_vec
    mean_term = jnp.mean(scaled, axis=-1, keepdims=True)
    cross_term = jnp.mean(scaled * normed, axis=-1, keepdims=True)
    return inverse_std * (scaled - mean_term - normed * cross_term)


def held_caption(own, part):
    return own ^ ((part & 1) * 8) ^ (part >> 1)


def caption_length(meta, caption):
    return meta[1 + caption]


def described_clip(meta, caption):
    return meta[17 + caption]


def row_of_y(own):
    return (own >> 1) & 3


def weight_of(w_ref, kind):
    rows = w_ref[:, kind * HEAD_DIM : (kind + 1) * HEAD_DIM, :]
    return rows.reshape(WIDTH, w_ref.shape[2])


def pack_kernel(*refs):
    count = len(refs) // 2 - 1
    blocks, out_ref, held, sems = refs[:count], refs[count], refs[count + 1 : -1], refs[-1]
    copies = [pltpu.make_async_copy(block, here, sems.at[k, HELD]) for k, (block, here) in enumerate(zip(blocks, held))]
    for copy in copies:
        copy.start()
    sent, first = [], 0
    for k, here in enumerate(held):
        copies[k].wait()
        for target in range(HELD):
            place = out_ref.at[target, pl.ds(first, here.shape[0])]
            sent.append(pltpu.make_async_copy(here, place, sems.at[k, target]))
            sent[-1].start()
        first += here.shape[0]
    for copy in sent:
        copy.wait()


def pack(name, *blocks):
    rows = sum(block.shape[0] for block in blocks)
    return pl.pallas_call(
        pack_kernel,
        out_shape=jax.ShapeDtypeStruct((HELD, rows, blocks[0].shape[1]), BF16),
        in_specs=[HBM] * len(blocks),
        out_specs=HBM,
        scratch_shapes=[pltpu.VMEM(block.shape, BF16) for block in blocks]
        + [pltpu.SemaphoreType.DMA((len(blocks), HELD + 1))],
        compiler_params=params(BIG),
        cost_estimate=COST,
        name=name,
    )(*blocks)


def norm_kernel(first, io, meta, t0, t1, gain, bias, hid_ref, up_ref):
    width = hid_ref.shape[1]
    io.take(0, 3, 4)
    own = meta[0]
    positions = lax.broadcasted_iota(jnp.int32, (CAP, 1), 0)
    gain_row, bias_row = gain[...].reshape(1, width), bias[...].reshape(1, width)
    for place, tokens in enumerate((t0, t1)):
        io.take(1 + place)
        span = slice(place * CAP, (place + 1) * CAP)
        normed, _ = standardize(tokens[0].astype(F32))
        hid_ref[span, :] = (normed * gain_row + bias_row).astype(BF16)
        live = positions < caption_length(meta, held_caption(own, first + 2 * place))
        up_ref[span, :] = jnp.where(live, tokens[1].astype(F32), 0.0).astype(BF16)


def segment_sum(values, ones):
    high = jnp.minimum(values, LARGEST_BF16).astype(BF16)
    low = (values - high.astype(F32)).astype(BF16)
    return dot(high, ones) + dot(low, ones)


def key_value_kernel(io, meta, gain, bias, kv_ref, near_ref, other_ref, out_ref, states_ref):
    width = states_ref.shape[1]
    io.take(0, 1, 2, 4, 5)
    own = meta[0]
    gain_row, bias_row = gain[...].reshape(1, width), bias[...].reshape(1, width)
    for part in range(HELD):
        clip = described_clip(meta, held_caption(own, part))
        place = row_of_y(clip) + 4 * ((clip ^ own) >> 3)
        near = ((clip ^ own) & 1) == 0
        frames = jnp.where(near, near_ref[place].astype(F32), other_ref[place].astype(F32))
        normed, _ = standardize(frames)
        states_ref[part * FRAMES : (part + 1) * FRAMES, :] = (normed * gain_row + bias_row).astype(BF16)
    io.take(3)
    for kind in range(2):
        out_ref[kind] = dot(states_ref[...], weight_of(kv_ref, kind), 1, 1).astype(BF16)


def join(target, near, far):
    for place in range(2):
        rows = slice(place * CAP, (place + 1) * CAP)
        target[2 * place * CAP : (2 * place + 1) * CAP, :] = near[rows, :]
        target[(2 * place + 1) * CAP : (2 * place + 2) * CAP, :] = far[rows, :]


def attend_kernel(io, kv_ref, qo_ref, h0, u0, h1, u1, dkv_ref, rows_ref):
    scale = 1.0 / math.sqrt(HEAD_DIM)
    pairs = HELD * FRAMES
    row_head = lax.broadcasted_iota(jnp.int32, (pairs, WIDTH), 0) // FRAMES
    lane_head = lax.broadcasted_iota(jnp.int32, (pairs, WIDTH), 1) // HEAD_DIM
    same = row_head == lane_head
    first = lax.broadcasted_iota(jnp.int32, (pairs, pairs), 0) // FRAMES
    second = lax.broadcasted_iota(jnp.int32, (pairs, pairs), 1) // FRAMES
    ones = jnp.where(first == second, 1.0, 0.0).astype(BF16)
    parts = range(HELD)
    spans = [slice(part * CAP, (part + 1) * CAP) for part in parts]

    def spread(rows):
        repeated = jnp.concatenate([rows.astype(F32)] * HELD, axis=0)
        return jnp.where(same, repeated, 0.0).astype(BF16)

    def collect(rows):
        kept = jnp.where(same, rows, 0.0)
        total = kept[0:FRAMES]
        for head in range(1, HELD):
            total = total + kept[head * FRAMES : (head + 1) * FRAMES]
        return total.astype(BF16)

    io.take(0)
    blocks = [[spread(kv_ref[kind, part * FRAMES : (part + 1) * FRAMES]) for part in parts] for kind in range(2)]
    keys, values = blocks
    io.take(1)

    def project(near, far, kind):
        found = []
        for place, rows_in in zip((2 + kind, 4 + kind), (near, far)):
            io.take(place)
            found.append(dot(rows_in[...], weight_of(qo_ref, kind), 1, 1).astype(BF16))
        return [found[part & 1][spans[part >> 1]] for part in parts]

    query = project(h0, h1, 0)
    d_att = project(u0, u1, 1)
    weights = [jnp.exp(dot(query[part], keys[part], 1, 1) * scale) for part in parts]
    d_softmax = [dot(d_att[part], values[part], 1, 1) for part in parts]
    sums = [segment_sum(weights[part], ones) for part in parts]
    softmax = [weights[part] / sums[part] for part in parts]
    low = [softmax[part].astype(BF16) for part in parts]
    inner = [segment_sum(softmax[part] * d_softmax[part], ones) for part in parts]
    d_values = [dot(low[part], d_att[part], 0, 0) for part in parts]
    d_scores = [(softmax[part] * (d_softmax[part] - inner[part]) * scale).astype(BF16) for part in parts]
    d_keys = [dot(d_scores[part], query[part], 0, 0) for part in parts]
    for kind, found in enumerate((d_keys, d_values)):
        for part in parts:
            block = collect(found[part])
            for row in range(HELD):
                dkv_ref[row, kind, part] = block
    io.give(0)
    for part in parts:
        rows_ref[0, spans[part], :] = dot(low[part], values[part]).astype(BF16)
        rows_ref[1, spans[part], :] = dot(d_scores[part], keys[part]).astype(BF16)


def product_kernel(
    io, rows_ref, h0, u0, h1, u1, qo_ref, grad_ref, send_x, send_update, send_rest, keep_ref, hid_ref, up_ref
):
    io.take(0, 1, 2, 3, 4)
    join(hid_ref, h0, h1)
    join(up_ref, u0, u1)
    half = hid_ref.shape[1] // 2
    for kind, right in enumerate((hid_ref, up_ref)):
        for side in range(2):
            product = dot(rows_ref[1 - kind], right[:, side * half : (side + 1) * half], 0, 0).astype(BF16)
            for head in range(HELD):
                grad_ref[side * HELD + head, kind * HEAD_DIM : (kind + 1) * HEAD_DIM, :] = product[
                    head * HEAD_DIM : (head + 1) * HEAD_DIM
                ]
    io.give(0)
    io.take(5)
    w_query, w_out = weight_of(qo_ref, 0), weight_of(qo_ref, 1)
    for part, (first, second) in enumerate(
        ((keep_ref.at[0], None), (keep_ref.at[1], None), (send_update, send_rest), (send_x, None))
    ):
        span = slice(part * CAP, (part + 1) * CAP)
        first[:CAP, :] = dot(rows_ref[0, span], w_out).astype(BF16)
        rest, start = (first, CAP) if second is None else (second, 0)
        rest[start : start + CAP, :] = dot(rows_ref[1, span], w_query).astype(BF16)
        rest[start + CAP :, :] = jnp.zeros((FRAMES, rest.shape[1]), BF16)


def state_kernel(meta_in, got_in, kv_in, *refs):
    send_x, send_rest, keep_ref, meta, got_ref, kv_ref, made, sems, keys_ref, values_ref = refs[3:]
    copies = [
        pltpu.make_async_copy(source, target, sems.at[place])
        for place, (source, target) in enumerate(((meta_in, meta), (got_in, got_ref), (kv_in, kv_ref)))
    ]
    for copy in copies:
        copy.start()
    for copy in copies:
        copy.wait()
    own = meta[0]
    for part in range(HELD):
        clip = held_caption(own, part)
        caption = 0
        for index in range(4 * HELD):
            caption = jnp.where(described_clip(meta, index) == clip, index, caption)
        row = row_of_y(caption)
        apart = caption ^ own
        place = (apart >> 3) + 2 * (apart & 1)
        keys_ref[part * FRAMES : (part + 1) * FRAMES, :] = got_ref[row, 0, place]
        values_ref[part * FRAMES : (part + 1) * FRAMES, :] = got_ref[row, 1, place]
    total = dot(keys_ref[...], weight_of(kv_ref, 0)) + dot(values_ref[...], weight_of(kv_ref, 1))
    copies = []
    for part in range(HELD):
        made[part] = total[part * FRAMES : (part + 1) * FRAMES].astype(BF16)
        target = (keep_ref.at[0], keep_ref.at[1], send_rest, send_x)[part]
        copies.append(
            pltpu.make_async_copy(made.at[part], target.at[pl.ds(target.shape[0] - FRAMES, FRAMES)], sems.at[3 + part])
        )
        copies[-1].start()
    for copy in copies:
        copy.wait()


def grad_sum_kernel(io, parts_ref, out_ref):
    io.take()
    total = parts_ref[0].astype(F32)
    for part in range(1, parts_ref.shape[0]):
        total = total + parts_ref[part].astype(F32)
    out_ref[...] = total.T.astype(BF16)


def grad_final_kernel(parts_ref, wq_ref, wo_ref):
    total = parts_ref[0].astype(F32)
    for part in range(1, parts_ref.shape[0]):
        total = total + parts_ref[part].astype(F32)
    wq_ref[...] = total[:, :HEAD_DIM]
    wo_ref[...] = total[:, HEAD_DIM:]


def add_kernel(io, left_ref, right_ref, out_ref):
    io.take()
    out_ref[...] = (left_ref[...].astype(F32) + right_ref[...].astype(F32)).astype(BF16)


def final_kernel(
    io,
    keep_ref,
    core_update,
    core_rest,
    x_ref,
    caption_ref,
    dec_gain,
    audio_ref,
    enc_gain,
    update_ref,
    grad_ref,
    out_ref,
):
    io.take()
    width = caption_ref.shape[1]

    def total(start, stop):
        core_ref, first = (core_update, 0) if start == 0 else (core_rest, CAP)
        near = keep_ref[start:stop].astype(F32) + core_ref[start - first : stop - first].astype(F32)
        return near + x_ref[start:stop].astype(F32)

    update_ref[...] = total(0, CAP).astype(BF16)
    io.give(0)
    normed, inverse_std = standardize(caption_ref[...].astype(F32))
    d_hidden = total(CAP, 2 * CAP)
    grad_ref[...] = norm_backward(d_hidden, normed, inverse_std, dec_gain[...].reshape(1, width)).astype(BF16)
    io.give(1)
    normed, inverse_std = standardize(audio_ref[0].astype(F32))
    d_states = total(2 * CAP, 2 * CAP + FRAMES)
    out_ref[0] = norm_backward(d_states, normed, inverse_std, enc_gain[...].reshape(1, width)).astype(BF16)


class Transfers:
    def __init__(self, takes, gives):
        self.takes, self.gives = dict(enumerate(takes)), dict(enumerate(gives))
        self.given = []
        for copy in takes:
            copy.start()

    def take(self, *places):
        for place in places or tuple(self.takes):
            self.takes.pop(place).wait()

    def give(self, *places):
        for place in places or tuple(self.gives):
            self.given.append(self.gives.pop(place))
            self.given[-1].start()

    def finish(self):
        if self.gives:
            self.give()
        for copy in self.given:
            copy.wait()


def call(kernel, name, outs, operands, mib=BIG, scratch=(), scalars=0):
    takes, gives = len(operands), len(outs)
    places = [operand[1] if isinstance(operand, tuple) else None for operand in operands]
    operands = [operand[0] if isinstance(operand, tuple) else operand for operand in operands]

    def copied(*refs):
        given, wanted, refs = refs[:takes], refs[takes : takes + gives], refs[takes + gives :]
        held, made, refs = refs[:takes], refs[takes : takes + gives], refs[takes + gives :]
        sems, rest = refs[0], refs[1:]
        io = Transfers(
            [
                pltpu.make_async_copy(
                    given[i] if places[i] is None else given[i].at[places[i]], held[i], sems.at[i]
                )
                for i in range(takes)
            ],
            [pltpu.make_async_copy(made[i], wanted[i], sems.at[takes + i]) for i in range(gives)],
        )
        kernel(io, *held, *made, *rest)
        io.finish()

    def space(place, array):
        shape = array.shape if places[place] is None else array.shape[1:]
        return (pltpu.SMEM if place < scalars else pltpu.VMEM)(shape, array.dtype)

    return pl.pallas_call(
        copied,
        out_shape=tuple(jax.ShapeDtypeStruct(*out) for out in outs),
        in_specs=[HBM] * takes,
        out_specs=(HBM,) * gives,
        scratch_shapes=[space(place, operand) for place, operand in enumerate(operands)]
        + [pltpu.VMEM(*out) for out in outs]
        + [pltpu.SemaphoreType.DMA((takes + gives,))]
        + list(scratch),
        compiler_params=params(mib),
        cost_estimate=COST,
        name=name,
    )(*operands)


def body(
    captions,
    audio,
    caption_len,
    pairing,
    enc_gain,
    enc_bias,
    dec_gain,
    dec_bias,
    w_query,
    w_key,
    w_value,
    w_out,
    grad_update,
    *,
    depth,
    y_groups,
    yx_groups,
    z_groups,
):
    both = ("dp", "mp")
    width = captions.shape[1]
    own = lax.axis_index("mp").astype(jnp.int32).reshape(1)
    meta = jnp.concatenate([own, caption_len, pairing[0], jnp.zeros((95,), jnp.int32)])
    swap_core = [(index, index ^ 1) for index in range(16)]
    swap_x = [(index, index ^ 8) for index in range(16)]

    kv_out = pack("pack_keys_values", w_key.T, w_value.T, audio.reshape(FRAMES, width))
    kv_got = lax.all_to_all(kv_out, "mp", 0, 0, axis_index_groups=y_groups, tiled=True)
    qo_out = pack("pack_queries_out", w_query.T, w_out)
    tokens_own = jnp.stack([captions, grad_update])
    tokens_x = lax.ppermute(tokens_own, "mp", swap_x)
    tokens_core = lax.ppermute(tokens_own, "mp", swap_core)

    def norms(first, name, near, other):
        return call(
            functools.partial(norm_kernel, first),
            name,
            [((2 * CAP, width), BF16), ((2 * CAP, width), BF16)],
            (meta, near, other, dec_gain, dec_bias),
            scalars=1,
        )

    normed_near = norms(0, "norms_near", tokens_own, tokens_core)
    kv_got, qo_out, *normed_near = lax.optimization_barrier((kv_got, qo_out, *normed_near))
    qo_got = lax.all_to_all(qo_out, "mp", 0, 0, axis_index_groups=y_groups, tiled=True)
    audio_y = kv_got[:, 2 * HEAD_DIM :]
    audio_near = jnp.concatenate([audio_y, lax.ppermute(audio_y, "mp", swap_x)])
    audio_other = lax.ppermute(audio_near, "mp", swap_core)
    (keys_values,) = call(
        key_value_kernel,
        "keys_values",
        [((2, HELD * FRAMES, WIDTH), BF16)],
        (meta, enc_gain, enc_bias, kv_got, audio_near, audio_other),
        scratch=[pltpu.VMEM((HELD * FRAMES, width), BF16)],
        scalars=1,
    )
    tokens_far = lax.ppermute(tokens_x, "mp", swap_core)
    normed_far = norms(1, "norms_far", tokens_x, tokens_far)

    d_kv, attended = call(
        attend_kernel,
        "attend",
        [((HELD, 2, HELD, FRAMES, WIDTH), BF16), ((2, ROWS, WIDTH), BF16)],
        (keys_values, qo_got, *normed_near, *normed_far),
    )
    d_kv_got = lax.all_to_all(d_kv, "mp", 0, 0, axis_index_groups=y_groups, tiled=True)
    rows = 2 * CAP + FRAMES
    weight_parts, send_x, send_update, *partials = call(
        product_kernel,
        "products",
        [
            ((2 * HELD, 2 * HEAD_DIM, width // 2), BF16),
            ((rows, width), BF16),
            ((CAP, width), BF16),
            ((rows - CAP, width), BF16),
            ((2, rows, width), BF16),
        ],
        (attended, *normed_near, *normed_far, qo_got),
        scratch=[pltpu.VMEM((ROWS, width), BF16)] * 2,
    )
    d_kv_got, weight_parts = lax.optimization_barrier((d_kv_got, weight_parts))
    weight_got = lax.all_to_all(weight_parts, both, 0, 0, axis_index_groups=yx_groups, tiled=True)
    partials = (send_x, *partials)
    send_x, send_rest, keep = pl.pallas_call(
        state_kernel,
        out_shape=tuple(jax.ShapeDtypeStruct(array.shape, BF16) for array in partials),
        in_specs=[HBM] * 6,
        out_specs=(HBM,) * 3,
        input_output_aliases={3 + place: place for place in range(3)},
        scratch_shapes=[
            pltpu.SMEM(meta.shape, meta.dtype),
            pltpu.VMEM(d_kv_got.shape, BF16),
            pltpu.VMEM(kv_got.shape, BF16),
            pltpu.VMEM((HELD, FRAMES, width), BF16),
            pltpu.SemaphoreType.DMA((3 + HELD,)),
        ]
        + [pltpu.VMEM((HELD * FRAMES, WIDTH), BF16)] * 2,
        compiler_params=params(BIG),
        cost_estimate=COST,
        name="state_grads",
    )(meta, d_kv_got, kv_got, *partials)
    core_x = lax.ppermute(send_x, "mp", swap_core)
    (x_out,) = call(add_kernel, "add_updates", [((rows, width), BF16)], ((keep, 1), core_x), mib=8)
    x_parts = lax.ppermute(x_out, "mp", swap_x)
    weight_got, _ = lax.optimization_barrier((weight_got, x_out))

    (weight_half,) = call(
        grad_sum_kernel, "sum_weight_grads", [((width // 2, 2 * HEAD_DIM), BF16)], (weight_got,), mib=8
    )
    weight_last = lax.all_to_all(
        weight_half.reshape(depth, width // (2 * depth), 2 * HEAD_DIM),
        both,
        0,
        0,
        axis_index_groups=z_groups,
        tiled=True,
    )
    send_update, send_rest, _ = lax.optimization_barrier((send_update, send_rest, weight_half))
    core_update = lax.ppermute(send_update, "mp", swap_core)
    core_rest = lax.ppermute(send_rest, "mp", swap_core)
    cross_update, grad_captions, grad_audio = call(
        final_kernel,
        "final_rows",
        [((CAP, width), BF16), ((CAP, width), BF16), ((1, FRAMES, width), BF16)],
        ((keep, 0), core_update, core_rest, x_parts, captions, dec_gain, audio, enc_gain),
        mib=16,
    )
    weight_last, cross_update, grad_captions, grad_audio = lax.optimization_barrier(
        (weight_last, cross_update, grad_captions, grad_audio)
    )
    rows = width // (2 * depth)
    grad_wq, grad_wo = pl.pallas_call(
        grad_final_kernel,
        out_shape=(jax.ShapeDtypeStruct((rows, HEAD_DIM), F32),) * 2,
        compiler_params=params(16),
        name="final_weight_grads",
    )(weight_last)
    return (cross_update, grad_captions, grad_audio, grad_wq, grad_wo.T)


def device_groups(dp_size):
    depth = dp_size // 2

    def device(x_hi, z, x_lo, y, core):
        return (x_hi * depth + z) * 16 + (x_lo * 4 + y) * 2 + core

    y_groups = [[(x * 4 + y) * 2 + core for y in range(4)] for x in range(2) for core in range(2)]
    yx_groups = [
        [device(x_hi, z, x_lo, y, core) for x_hi in range(2) for y in range(4)]
        for z in range(depth)
        for x_lo in range(2)
        for core in range(2)
    ]
    z_groups = [
        [device(x_hi, z, x_lo, y, core) for z in range(depth)]
        for x_hi in range(2)
        for x_lo in range(2)
        for y in range(4)
        for core in range(2)
    ]
    return dict(depth=depth, y_groups=y_groups, yx_groups=yx_groups, z_groups=z_groups)


def solution(mesh):
    in_specs = (
        P(("dp", "mp"), None),
        P(("dp", "mp"), None, None),
        P("dp"),
        P("dp", None),
        P(),
        P(),
        P(),
        P(),
        P(None, "mp"),
        P(None, "mp"),
        P(None, "mp"),
        P("mp", None),
        P(("dp", "mp"), None),
    )
    out_specs = (
        P(("dp", "mp"), None),
        P(("dp", "mp"), None),
        P(("dp", "mp"), None, None),
        P("dp", "mp"),
        P("mp", "dp"),
    )
    local = functools.partial(body, **device_groups(mesh.shape["dp"]))
    return jax.shard_map(local, mesh=mesh, in_specs=in_specs, out_specs=out_specs, check_vma=False)
```
